1024 devices in a mesh: rep: 8 (over x, core), shard: 128 (over z, y).
Axes of the slice: x: 4, y: 4, z: 32, core: 2. Of those that a mesh axis runs over, the one named last changes fastest.
Arguments:
- partial_grads: bfloat16 [8, 8, 7168, 576], P('rep', None, 'shard'), may hold values from -1440 to 1440
- momentum: float32 [8, 7168, 576], P('rep', 'shard'), may hold values from -6 to 6
Outputs:
- update: bfloat16 [8, 7168, 576], P(None, 'shard')
- new_momentum: float32 [8, 7168, 576], P('rep', 'shard')
The draws below stay inside these ranges and needn't reach their ends.
All inputs are finite; a program needn't handle non-finite values.
Results may differ from the reference program's by a relative error of at most 0.0056.
The reference program's roundings to bfloat16 on the way count: a program that leaves them out, or rounds other values in their place, can miss the bound.
Values may be sent and summed in bfloat16 or wider, within the bound.
No kernel may reach another device: no remote copies, remote signals or barrier semaphores. Data moves between devices by JAX's collectives and lax.ppermute only.
A program may use at most 32 MiB of HBM per device.

```python
import math
import jax
import jax.numpy as jnp
from jax import lax

D = 7168
KV = 576
ITERS = 2
MATRICES = 8
N_REP = 8
N_SHARD = 128


def draw_partial_grads(key, part):
    key = jax.random.fold_in(key, 11)
    key_rows = jax.random.fold_in(key, 0)
    key_cols = jax.random.fold_in(key, 1)
    key_reps = jax.random.fold_in(key, 2)
    key_base = jax.random.fold_in(key, 3)
    key_pair = jax.random.fold_in(key, 5)
    key_left = jax.random.fold_in(key, 6)
    key_right = jax.random.fold_in(key, 7)
    row_pos = jnp.arange(D, dtype=jnp.float32) / D
    row_scale = jnp.exp(jnp.log(3.0) * row_pos)[None, :] * jnp.exp(jax.random.uniform(key_rows, (MATRICES, D), minval=0.0, maxval=jnp.log(10.0)))
    col_scale = jnp.exp(jax.random.uniform(key_cols, (MATRICES, KV), minval=0.0, maxval=jnp.log(10.0)))
    rep_scale = jnp.exp(jax.random.uniform(key_reps, (N_REP, 1, 1, 1), minval=0.0, maxval=jnp.log(3.0)))
    pairing = jax.random.permutation(key_pair, N_SHARD)
    row_block = jnp.arange(D) // (D // N_SHARD)
    col_share = (KV + N_SHARD - 1) // N_SHARD
    col_block = jnp.arange(KV) // col_share
    spike = jnp.where(pairing[row_block][:, None] == col_block[None, :], 8.0, 1.0)
    base_draw = jnp.clip(jax.random.normal(key_base, (N_REP, MATRICES, D, KV)), -4.0, 4.0)
    left = jnp.clip(jax.random.normal(key_left, (2, MATRICES, D)), -3.0, 3.0)
    right = jnp.clip(jax.random.normal(key_right, (2, MATRICES, KV)), -3.0, 3.0)
    shared_amp = 0.3
    shared = left[0][:, :, None] * right[0][:, None, :] + left[1][:, :, None] * right[1][:, None, :]
    mixed = jnp.clip(base_draw + shared_amp * shared[None], -4.0, 4.0)
    values = 0.05 * mixed * rep_scale * row_scale[None, :, :, None] * col_scale[None, :, None, :] * spike[None, None, :, :]
    return values.astype(jnp.bfloat16)


def shard_levels(own_key, extent, cuts, low, top_value):
    level, own = 1.0, jax.random.fold_in(own_key, 6)
    for axis_at, blocks in cuts:
        draws = jnp.exp(jax.random.uniform(jax.random.fold_in(own, axis_at), (blocks,), jnp.float32, low / len(cuts), top_value / len(cuts)))
        level = level * jnp.repeat(draws, extent[axis_at] // blocks).reshape([-1 if axis == axis_at else 1 for axis in range(len(extent))])
    return level


def noise(stream_key, shape, width, limit, cuts=(), kind=jnp.bfloat16):
    drawn = jax.random.normal(stream_key, shape, jnp.float32) * width
    if len(cuts) > 0:
        drawn = shard_levels(stream_key, shape, cuts, -0.22, 0.18) * drawn
    return jnp.clip(drawn, min=-limit, max=limit).astype(kind)


def setup_inputs(seed: int = 0) -> dict:
    key_of = jax.random.split(jax.random.key(seed), 3)
    return {
        "partial_grads": draw_partial_grads(jax.random.fold_in(key_of[2], 71), 0),
        "momentum": noise(key_of[1], (MATRICES, D, KV), 1.0, 6.0, ((0, 8), (1, 128)), jnp.float32),
    }


linear_coeff = 3.4445
cubic_coeff = -4.775
quintic_coeff = 2.0315
momentum_rate = 0.9
norm_eps = 1e-06

def newton(velocity):
    total_squares = jnp.sum(jnp.square(velocity.astype(jnp.float32)))
    inv_norm = 1.0 / (jnp.sqrt(total_squares) + norm_eps)
    factor = 0.2 * math.sqrt(max(D, KV))
    current = velocity
    for iteration in range(ITERS):
        gram_full = jnp.dot(current.T, current, preferred_element_type=jnp.float32)
        if iteration == 0:
            gram_full = gram_full * (inv_norm * inv_norm)
        gram_b = lax.optimization_barrier(gram_full.astype(jnp.bfloat16))
        poly_term = (cubic_coeff * gram_b.astype(jnp.float32) + quintic_coeff * jnp.dot(gram_b, gram_b, preferred_element_type=jnp.float32)).astype(jnp.bfloat16)
        next_iter = linear_coeff * current.astype(jnp.float32) + jnp.dot(current, poly_term, preferred_element_type=jnp.float32)
        if iteration == 0:
            next_iter = next_iter * inv_norm
        if iteration == ITERS - 1:
            next_iter = next_iter * factor
        current = next_iter.astype(jnp.bfloat16)
    return current

def reference(partial_grads, momentum):
    summed = lax.optimization_barrier(jnp.sum(partial_grads.astype(jnp.float32), axis=0))
    new_momentum = momentum_rate * momentum + summed
    velocity = (summed + momentum_rate * new_momentum).astype(jnp.bfloat16)
    update = lax.map(newton, velocity)
    return (update, new_momentum)
```

```python
import functools
import math

import jax
import jax.numpy as jnp
import numpy as np
from jax import lax
from jax.experimental import pallas as pl
from jax.experimental.pallas import tpu as pltpu
from jax.sharding import Mesh
from jax.sharding import PartitionSpec as P

linear_coeff = 3.4445
cubic_coeff = -4.775
quintic_coeff = 2.0315
momentum_rate = 0.9
norm_eps = 1e-06

TILE = 128
TILES = 5
WIDE = TILE * TILES
SLOTS = 4


def slot_tiles(y):
    return [
        (y, 4),
        (y, y),
        (y, (y + 1) % 4),
        [(0, 2), (1, 3), (4, 4), None][y],
    ]


def dot_tn(a, b):
    return lax.dot_general(a, b, (((0,), (0,)), ((), ())), preferred_element_type=jnp.float32)


def gram_kernel(rows_ref, out_ref):
    y = lax.axis_index("y")
    last = jnp.where(y < 2, y, 4)
    left = [y, y, y, last]
    right = [4, y, lax.rem(y + 1, 4), jnp.where(y < 2, y + 2, 4)]
    for slot in range(SLOTS):
        at = pl.ds(pl.multiple_of(left[slot] * TILE, TILE), TILE)
        to = pl.ds(pl.multiple_of(right[slot] * TILE, TILE), TILE)
        total = dot_tn(rows_ref[0, :, at], rows_ref[0, :, to])
        for part in range(1, rows_ref.shape[0]):
            total += dot_tn(rows_ref[part, :, at], rows_ref[part, :, to])
        tile = total.astype(out_ref.dtype)
        height = out_ref.shape[1]
        per = TILE // height
        for piece in range(per):
            out_ref[slot * per + piece] = tile[piece * height : (piece + 1) * height]


def sum_kernel(parts_ref, out_ref):
    total = parts_ref[0].astype(jnp.float32)
    for part in range(1, parts_ref.shape[0]):
        total += parts_ref[part].astype(jnp.float32)
    rounded = total.astype(out_ref.dtype)
    for part in range(out_ref.shape[0]):
        out_ref[part] = rounded


def newton_kernel(factor, tiles_ref, rows_ref, out_ref, gram, work, poly):
    total = jnp.float32(0.0)
    row = lax.broadcasted_iota(jnp.int32, (TILE, TILE), 0)
    col = lax.broadcasted_iota(jnp.int32, (TILE, TILE), 1)
    for y in range(4):
        for slot, place in enumerate(slot_tiles(y)):
            if place is None:
                continue
            i, j = place
            tile = tiles_ref[y, slot * TILE : (slot + 1) * TILE, :]
            gram[i * TILE : (i + 1) * TILE, j * TILE : (j + 1) * TILE] = tile
            wide = tile.astype(jnp.float32)
            if i == j:
                total += jnp.sum(jnp.where(row == col, wide, 0.0))
            else:
                gram[j * TILE : (j + 1) * TILE, i * TILE : (i + 1) * TILE] = wide.T.astype(gram.dtype)
    total = jnp.full((1, 1), total, jnp.float32)
    inv_norm = 1.0 / (jnp.sqrt(total) + norm_eps)
    inv_square = inv_norm * inv_norm

    def dot(a, b):
        return jnp.dot(a, b, preferred_element_type=jnp.float32)

    g = gram[...]
    square = dot(g, g) * inv_square
    poly[...] = (
        (cubic_coeff * g.astype(jnp.float32) + quintic_coeff * square) * inv_square
    ).astype(poly.dtype)
    half = (linear_coeff * g.astype(jnp.float32) + dot(g, poly[...])) * inv_square
    work[...] = half.astype(work.dtype)
    second = (linear_coeff * half + dot(poly[...], work[...])).astype(gram.dtype)

    rows = rows_ref[...]
    first = (linear_coeff * rows.astype(jnp.float32) + dot(rows, poly[...])) * inv_norm
    first = first.astype(jnp.bfloat16)

    gram[...] = second
    g = gram[...]
    work[...] = (
        cubic_coeff * g.astype(jnp.float32) + quintic_coeff * dot(g, g)
    ).astype(work.dtype)
    result = linear_coeff * first.astype(jnp.float32) + dot(first, work[...])
    out_ref[...] = (result * factor)[:, : out_ref.shape[1]].astype(out_ref.dtype)


def vmem(n):
    return [pl.BlockSpec(memory_space=pltpu.VMEM)] * n


def call(kernel, out, n_in, scratch=()):
    return pl.pallas_call(
        kernel,
        out_shape=jax.ShapeDtypeStruct(out, jnp.bfloat16),
        in_specs=vmem(n_in),
        out_specs=vmem(1)[0],
        scratch_shapes=[pltpu.VMEM(s, jnp.bfloat16) for s in scratch],
        compiler_params=pltpu.CompilerParams(vmem_limit_bytes=32 * 1024 * 1024),
    )


def local(partial_grads, momentum):
    rep = ("x", "core")
    planes, lanes = lax.axis_size("z"), lax.axis_size("y")
    received = lax.all_to_all(partial_grads[0], rep, 0, 0, tiled=True)
    summed = jnp.sum(received.astype(jnp.float32), axis=0)
    new_momentum = momentum_rate * momentum[0] + summed
    velocity = (summed + momentum_rate * new_momentum).astype(jnp.bfloat16)
    row_count, kv_width = velocity.shape
    factor = 0.2 * math.sqrt(max(row_count * planes * lanes, kv_width))

    wide = jnp.pad(velocity, ((0, 0), (0, WIDE - kv_width)))
    spread = jnp.broadcast_to(wide[None], (lanes, row_count, WIDE))
    plane_rows = lax.all_to_all(spread, "y", 0, 0, tiled=True)

    chunk = (planes, SLOTS * TILE // planes, TILE)
    parts = call(gram_kernel, chunk, 1)(plane_rows)
    parts = lax.all_to_all(parts, "z", 0, 0, tiled=True)
    shares = call(sum_kernel, chunk, 1)(parts)
    shares = lax.all_to_all(shares, "z", 0, 0, tiled=True)
    quarter = shares.reshape(SLOTS * TILE, TILE)
    quarters = lax.all_to_all(
        jnp.broadcast_to(quarter[None], (lanes, SLOTS * TILE, TILE)), "y", 0, 0, tiled=True
    )
    update = call(
        functools.partial(newton_kernel, factor), (row_count, kv_width), 2, [(WIDE, WIDE)] * 3
    )(quarters, wide)
    update = lax.all_gather(update, rep, axis=0, tiled=False)
    return (update, new_momentum[None])


def solution(mesh):
    devices = np.asarray(mesh.devices)
    fine = Mesh(devices.reshape(4, 2, 32, 4), ("x", "core", "z", "y"))
    rep, shard = ("x", "core"), ("z", "y")
    return jax.shard_map(
        local,
        mesh=fine,
        in_specs=(P(rep, None, shard, None), P(rep, shard, None)),
        out_specs=(P(None, shard, None), P(rep, shard, None)),
        check_vma=False,
    )
```

```python
import functools
import math

import jax
import jax.numpy as jnp
import numpy as np
from jax import lax
from jax.experimental import pallas as pl
from jax.experimental.pallas import tpu as pltpu
from jax.sharding import Mesh
from jax.sharding import PartitionSpec as P

linear_coeff = 3.4445
cubic_coeff = -4.775
quintic_coeff = 2.0315
momentum_rate = 0.9
norm_eps = 1e-06

TILE = 128
HALF = 64
TILES = 5
WIDE = TILE * TILES
PACKED = 384


def dot_tn(a, b):
    return lax.dot_general(a, b, (((0,), (0,)), ((), ())), preferred_element_type=jnp.float32)


def left_half(rows):
    return lax.broadcasted_iota(jnp.int32, (rows, TILE), 1) < HALF


def gram_kernel(rows_ref, out_ref):
    y = lax.axis_index("y")

    def tile(i, j):
        at = pl.ds(pl.multiple_of(i * TILE, TILE), TILE)
        to = pl.ds(pl.multiple_of(j * TILE, TILE), TILE)
        total = dot_tn(rows_ref[0, :, at], rows_ref[0, :, to])
        for part in range(1, rows_ref.shape[0]):
            total += dot_tn(rows_ref[part, :, at], rows_ref[part, :, to])
        return total

    far = lax.rem(y, 2)
    split = tile(far, far + 2)
    diagonal = tile(y, y)
    out_ref[0:128, :] = tile(y, lax.rem(y + 1, 4)).astype(out_ref.dtype)
    out_ref[128:192, :] = jnp.where(y < 2, split[:HALF], split[HALF:]).astype(out_ref.dtype)
    out_ref[192:256, :] = tile(4, y)[:HALF].astype(out_ref.dtype)
    out_ref[256:320, :] = diagonal[:HALF].astype(out_ref.dtype)
    corner = jnp.where(left_half(HALF), tile(4, 4)[:HALF], diagonal[HALF:])
    out_ref[320:384, :] = corner.astype(out_ref.dtype)


def sum_kernel(parts_ref, out_ref):
    total = parts_ref[0].astype(jnp.float32)
    for part in range(1, parts_ref.shape[0]):
        total += parts_ref[part].astype(jnp.float32)
    rounded = total.astype(out_ref.dtype)
    for part in range(out_ref.shape[0]):
        out_ref[part] = rounded


def newton_kernel(factor, packed_ref, rows_ref, out_ref, gram, work, poly):
    zeros = jnp.zeros((HALF, TILE), jnp.float32)
    row = lax.broadcasted_iota(jnp.int32, (HALF, TILE), 0)
    col = lax.broadcasted_iota(jnp.int32, (HALF, TILE), 1)
    trace = zeros

    def part(y, start, stop):
        return packed_ref[y, start:stop, :].astype(jnp.float32)

    def put(i, j, tile):
        gram[i * TILE : (i + 1) * TILE, j * TILE : (j + 1) * TILE] = tile.astype(gram.dtype)

    def put_both(i, j, tile):
        put(i, j, tile)
        put(j, i, tile.T)

    for y in range(4):
        put_both(y, (y + 1) % 4, part(y, 0, 128))
        put_both(4, y, jnp.concatenate([part(y, 192, 256), zeros], axis=0))
        upper, corner = part(y, 256, 320), part(y, 320, 384)
        mirrored = jnp.concatenate([upper, zeros], axis=0).T
        lower = jnp.where(left_half(HALF), mirrored[HALF:], corner)
        put(y, y, jnp.concatenate([upper, lower], axis=0))
        trace += jnp.where(row == col, upper, 0.0) + jnp.where(row + HALF == col, corner, 0.0)
        if y == 0:
            trace += jnp.where(row == col, corner, 0.0)
            last = jnp.where(left_half(HALF), corner, 0.0)
            put(4, 4, jnp.concatenate([last, zeros], axis=0))
    for i in range(2):
        put_both(i, i + 2, jnp.concatenate([part(i, 128, 192), part(i + 2, 128, 192)], axis=0))

    total = jnp.sum(trace, axis=(0, 1), keepdims=True)
    inv_norm = 1.0 / (jnp.sqrt(total) + norm_eps)
    inv_square = inv_norm * inv_norm

    def dot(a, b):
        return jnp.dot(a, b, preferred_element_type=jnp.float32)

    g = gram[...]
    square = dot(g, g) * inv_square
    poly[...] = (
        (cubic_coeff * g.astype(jnp.float32) + quintic_coeff * square) * inv_square
    ).astype(poly.dtype)
    half = (linear_coeff * g.astype(jnp.float32) + dot(g, poly[...])) * inv_square
    work[...] = half.astype(work.dtype)
    second = (linear_coeff * half + dot(poly[...], work[...])).astype(gram.dtype)

    rows = rows_ref[...]
    first = (linear_coeff * rows.astype(jnp.float32) + dot(rows, poly[...])) * inv_norm
    first = first.astype(jnp.bfloat16)

    gram[...] = second
    g = gram[...]
    work[...] = (
        cubic_coeff * g.astype(jnp.float32) + quintic_coeff * dot(g, g)
    ).astype(work.dtype)
    result = linear_coeff * first.astype(jnp.float32) + dot(first, work[...])
    out_ref[...] = (result * factor)[:, : out_ref.shape[1]].astype(out_ref.dtype)


def vmem(n):
    return [pl.BlockSpec(memory_space=pltpu.VMEM)] * n


def call(kernel, out, n_in, scratch=()):
    return pl.pallas_call(
        kernel,
        out_shape=jax.ShapeDtypeStruct(out, jnp.bfloat16),
        in_specs=vmem(n_in),
        out_specs=vmem(1)[0],
        scratch_shapes=[pltpu.VMEM(s, jnp.bfloat16) for s in scratch],
        compiler_params=pltpu.CompilerParams(vmem_limit_bytes=32 * 1024 * 1024),
    )


def local(partial_grads, momentum):
    rep = ("x", "core")
    lanes, blocks, near = lax.axis_size("y"), lax.axis_size("block"), lax.axis_size("near")
    received = lax.all_to_all(partial_grads[0], rep, 0, 0, tiled=True)
    summed = jnp.sum(received.astype(jnp.float32), axis=0)
    new_momentum = momentum_rate * momentum[0] + summed
    velocity = (summed + momentum_rate * new_momentum).astype(jnp.bfloat16)
    row_count, kv_width = velocity.shape
    factor = 0.2 * math.sqrt(max(row_count * blocks * near * lanes, kv_width))

    wide = jnp.pad(velocity, ((0, 0), (0, WIDE - kv_width)))
    spread = jnp.broadcast_to(wide[None], (lanes, row_count, WIDE))
    plane_rows = lax.all_to_all(spread, "y", 0, 0, tiled=True)

    share = PACKED // near
    parts = call(gram_kernel, (PACKED, TILE), 1)(plane_rows).reshape(near, share, TILE)
    parts = lax.all_to_all(parts, "near", 0, 0, tiled=True)
    parts = call(sum_kernel, (blocks, share, TILE), 1)(parts)
    parts = lax.all_to_all(parts, "block", 0, 0, tiled=True)
    parts = call(sum_kernel, (near, share, TILE), 1)(parts)
    parts = lax.all_to_all(parts, "near", 0, 0, tiled=True)
    packed = jnp.broadcast_to(parts.reshape(1, PACKED, TILE), (lanes, PACKED, TILE))
    packed = lax.all_to_all(packed, "y", 0, 0, tiled=True)
    update = call(
        functools.partial(newton_kernel, factor), (row_count, kv_width), 2, [(WIDE, WIDE)] * 3
    )(packed, wide)
    update = lax.all_gather(update, rep, axis=0, tiled=False)
    return (update, new_momentum[None])


def solution(mesh):
    devices = np.asarray(mesh.devices)
    fine = Mesh(devices.reshape(4, 2, 4, 8, 4), ("x", "core", "block", "near", "y"))
    rep, shard = ("x", "core"), ("block", "near", "y")
    return jax.shard_map(
        local,
        mesh=fine,
        in_specs=(P(rep, None, shard, None), P(rep, shard, None)),
        out_specs=(P(None, shard, None), P(rep, shard, None)),
        check_vma=False,
    )
```

```python
import functools
import math

import jax
import jax.numpy as jnp
import numpy as np
from jax import lax
from jax.experimental import pallas as pl
from jax.experimental.pallas import tpu as pltpu
from jax.sharding import Mesh
from jax.sharding import PartitionSpec as P

linear_coeff = 3.4445
cubic_coeff = -4.775
quintic_coeff = 2.0315
momentum_rate = 0.9
norm_eps = 1e-06

TILE = 128
HALF = 64
TILES = 5
WIDE = TILE * TILES
GROUPS = 4
PACKED = 384


def left_half(rows):
    return lax.broadcasted_iota(jnp.int32, (rows, TILE), 1) < HALF


def gram_kernel(
    received_ref, momentum_ref, wide_ref, packed_ref, new_ref, momentum, new, read_done, write_done
):
    read = pltpu.make_async_copy(momentum_ref, momentum, read_done)
    read.start()
    summed = received_ref[0].astype(jnp.float32)
    for part in range(1, received_ref.shape[0]):
        summed += received_ref[part].astype(jnp.float32)
    read.wait()
    updated = momentum_rate * momentum[...] + summed
    new[...] = updated
    write = pltpu.make_async_copy(new, new_ref, write_done)
    write.start()
    velocity = (summed + momentum_rate * updated).astype(wide_ref.dtype)
    rows, width = velocity.shape
    padding = jnp.zeros((rows, WIDE - width), wide_ref.dtype)
    wide_ref[...] = jnp.concatenate([velocity, padding], axis=1)

    def tile(i, j):
        return lax.dot_general(
            wide_ref[:, i * TILE : (i + 1) * TILE],
            wide_ref[:, j * TILE : (j + 1) * TILE],
            (((0,), (0,)), ((), ())),
            preferred_element_type=jnp.float32,
        )

    def put(start, block):
        packed_ref[start : start + block.shape[0], :] = block.astype(packed_ref.dtype)

    last = tile(4, 4)[:HALF]
    for y in range(GROUPS):
        base = y * PACKED
        put(base, tile(y, (y + 1) % 4))
        put(base + 192, tile(4, y)[:HALF])
        diagonal = tile(y, y)
        put(base + 256, diagonal[:HALF])
        put(base + 320, jnp.where(left_half(HALF), last, diagonal[HALF:]))
    for i in range(2):
        split = tile(i, i + 2)
        put(i * PACKED + 128, split[:HALF])
        put((i + 2) * PACKED + 128, split[HALF:])
    write.wait()


def sum_kernel(parts_ref, out_ref):
    total = parts_ref[0].astype(jnp.float32)
    for part in range(1, parts_ref.shape[0]):
        total += parts_ref[part].astype(jnp.float32)
    rounded = total.astype(out_ref.dtype)
    for part in range(out_ref.shape[0]):
        out_ref[part] = rounded


def newton_kernel(factor, packed_ref, rows_ref, out_ref, gram, work, poly):
    zeros = jnp.zeros((HALF, TILE), jnp.float32)
    row = lax.broadcasted_iota(jnp.int32, (HALF, TILE), 0)
    col = lax.broadcasted_iota(jnp.int32, (HALF, TILE), 1)
    trace = zeros

    def part(y, start, stop):
        return packed_ref[y * PACKED + start : y * PACKED + stop, :].astype(jnp.float32)

    def put(i, j, tile):
        gram[i * TILE : (i + 1) * TILE, j * TILE : (j + 1) * TILE] = tile.astype(gram.dtype)

    def put_both(i, j, tile):
        put(i, j, tile)
        put(j, i, tile.T)

    for y in range(GROUPS):
        put_both(y, (y + 1) % 4, part(y, 0, 128))
        put_both(4, y, jnp.concatenate([part(y, 192, 256), zeros], axis=0))
        upper, corner = part(y, 256, 320), part(y, 320, 384)
        mirrored = jnp.concatenate([upper, zeros], axis=0).T
        lower = jnp.where(left_half(HALF), mirrored[HALF:], corner)
        put(y, y, jnp.concatenate([upper, lower], axis=0))
        trace += jnp.where(row == col, upper, 0.0) + jnp.where(row + HALF == col, corner, 0.0)
        if y == 0:
            trace += jnp.where(row == col, corner, 0.0)
            last = jnp.where(left_half(HALF), corner, 0.0)
            put(4, 4, jnp.concatenate([last, zeros], axis=0))
    for i in range(2):
        put_both(i, i + 2, jnp.concatenate([part(i, 128, 192), part(i + 2, 128, 192)], axis=0))

    total = jnp.sum(trace, axis=(0, 1), keepdims=True)
    inv_norm = 1.0 / (jnp.sqrt(total) + norm_eps)
    inv_square = inv_norm * inv_norm

    def dot(a, b):
        return jnp.dot(a, b, preferred_element_type=jnp.float32)

    g = gram[...]
    square = dot(g, g) * inv_square
    poly[...] = (
        (cubic_coeff * g.astype(jnp.float32) + quintic_coeff * square) * inv_square
    ).astype(poly.dtype)
    half = (linear_coeff * g.astype(jnp.float32) + dot(g, poly[...])) * inv_square
    work[...] = half.astype(work.dtype)
    second = (linear_coeff * half + dot(poly[...], work[...])).astype(gram.dtype)

    rows = rows_ref[...]
    first = (linear_coeff * rows.astype(jnp.float32) + dot(rows, poly[...])) * inv_norm
    first = first.astype(jnp.bfloat16)

    gram[...] = second
    g = gram[...]
    work[...] = (
        cubic_coeff * g.astype(jnp.float32) + quintic_coeff * dot(g, g)
    ).astype(work.dtype)
    result = linear_coeff * first.astype(jnp.float32) + dot(first, work[...])
    out_ref[...] = (result * factor)[:, : out_ref.shape[1]].astype(out_ref.dtype)


VMEM = pl.BlockSpec(memory_space=pltpu.VMEM)
HBM = pl.BlockSpec(memory_space=pl.ANY)
PARAMS = pltpu.CompilerParams(vmem_limit_bytes=32 * 1024 * 1024)


def bf16(*shape):
    return jax.ShapeDtypeStruct(shape, jnp.bfloat16)


def gram(received, momentum):
    rows = momentum.shape[0]
    return pl.pallas_call(
        gram_kernel,
        out_shape=(
            bf16(rows, WIDE),
            bf16(GROUPS * PACKED, TILE),
            jax.ShapeDtypeStruct(momentum.shape, momentum.dtype),
        ),
        in_specs=[VMEM, HBM],
        out_specs=(VMEM, VMEM, HBM),
        scratch_shapes=[pltpu.VMEM(momentum.shape, momentum.dtype)] * 2
        + [pltpu.SemaphoreType.DMA] * 2,
        compiler_params=PARAMS,
    )(received, momentum)


def total_of(parts, receivers):
    return pl.pallas_call(
        sum_kernel,
        out_shape=bf16(receivers, *parts.shape[1:]),
        in_specs=[VMEM],
        out_specs=VMEM,
        compiler_params=PARAMS,
    )(parts)


def newton(factor, packed, wide, width):
    return pl.pallas_call(
        functools.partial(newton_kernel, factor),
        out_shape=bf16(wide.shape[0], width),
        in_specs=[VMEM, VMEM],
        out_specs=VMEM,
        scratch_shapes=[pltpu.VMEM((WIDE, WIDE), jnp.bfloat16)] * 3,
        compiler_params=PARAMS,
    )(packed, wide)


def local(partial_grads, momentum):
    rep, cluster = ("x", "core"), ("near", "y")
    blocks = lax.axis_size("block")
    members = lax.axis_size(cluster)
    row_count, kv_width = momentum.shape[1:]
    factor = 0.2 * math.sqrt(max(row_count * blocks * members, kv_width))

    received = lax.all_to_all(partial_grads[0], rep, 0, 0, tiled=True)
    wide, packed, new_momentum = gram(received, momentum[0])

    packed = packed.reshape(members, GROUPS * PACKED // members, TILE)
    packed = lax.all_to_all(packed, cluster, 0, 0, tiled=True)
    packed = lax.all_to_all(total_of(packed, blocks), "block", 0, 0, tiled=True)
    packed = lax.all_to_all(total_of(packed, members), cluster, 0, 0, tiled=True)
    packed = packed.reshape(GROUPS * PACKED, TILE)

    update = newton(factor, packed, wide, kv_width)
    update = lax.all_gather(update, rep, axis=0, tiled=False)
    return (update, new_momentum[None])


def solution(mesh):
    devices = np.asarray(mesh.devices)
    fine = Mesh(devices.reshape(4, 2, 8, 4, 4), ("x", "core", "block", "near", "y"))
    rep, shard = ("x", "core"), ("block", "near", "y")
    return jax.shard_map(
        local,
        mesh=fine,
        in_specs=(P(rep, None, shard, None), P(rep, shard, None)),
        out_specs=(P(None, shard, None), P(rep, shard, None)),
        check_vma=False,
    )
```

```python
import functools
import math

import jax
import jax.numpy as jnp
import numpy as np
from jax import lax
from jax.experimental import pallas as pl
from jax.experimental.pallas import tpu as pltpu
from jax.sharding import Mesh
from jax.sharding import PartitionSpec as P

linear_coeff = 3.4445
cubic_coeff = -4.775
quintic_coeff = 2.0315
momentum_rate = 0.9
norm_eps = 1e-06

TILE = 128
HALF = 64
TILES = 5
WIDE = TILE * TILES
GROUPS = 4
PACKED = 384


def left_half(rows):
    return lax.broadcasted_iota(jnp.int32, (rows, TILE), 1) < HALF


def gram_kernel(
    received_ref, momentum_ref, wide_ref, packed_ref, new_ref, momentum, new, read_done, write_done
):
    read = pltpu.make_async_copy(momentum_ref, momentum, read_done)
    read.start()
    summed = received_ref[0].astype(jnp.float32)
    for part in range(1, received_ref.shape[0]):
        summed += received_ref[part].astype(jnp.float32)
    read.wait()
    updated = momentum_rate * momentum[...] + summed
    new[...] = updated
    write = pltpu.make_async_copy(new, new_ref, write_done)
    write.start()
    velocity = (summed + momentum_rate * updated).astype(wide_ref.dtype)
    rows, width = velocity.shape
    padding = jnp.zeros((rows, WIDE - width), wide_ref.dtype)
    wide_ref[...] = jnp.concatenate([velocity, padding], axis=1)

    def tile(i, j):
        return lax.dot_general(
            wide_ref[:, i * TILE : (i + 1) * TILE],
            wide_ref[:, j * TILE : (j + 1) * TILE],
            (((0,), (0,)), ((), ())),
            preferred_element_type=jnp.float32,
        )

    def put(start, block):
        packed_ref[start : start + block.shape[0], :] = block.astype(packed_ref.dtype)

    last = tile(4, 4)[:HALF]
    for y in range(GROUPS):
        base = y * PACKED
        put(base, tile(y, (y + 1) % 4))
        put(base + 192, tile(4, y)[:HALF])
        diagonal = tile(y, y)
        put(base + 256, diagonal[:HALF])
        put(base + 320, jnp.where(left_half(HALF), last, diagonal[HALF:]))
    for i in range(2):
        split = tile(i, i + 2)
        put(i * PACKED + 128, split[:HALF])
        put((i + 2) * PACKED + 128, split[HALF:])
    write.wait()


def sum_kernel(parts_ref, out_ref):
    total = parts_ref[0].astype(jnp.float32)
    for part in range(1, parts_ref.shape[0]):
        total += parts_ref[part].astype(jnp.float32)
    rounded = total.astype(out_ref.dtype)
    for part in range(out_ref.shape[0]):
        out_ref[part] = rounded


def newton_kernel(factor, packed_ref, rows_ref, out_ref, gram, work, poly):
    zeros = jnp.zeros((HALF, TILE), jnp.float32)
    row = lax.broadcasted_iota(jnp.int32, (HALF, TILE), 0)
    col = lax.broadcasted_iota(jnp.int32, (HALF, TILE), 1)
    trace = zeros

    def part(y, start, stop):
        return packed_ref[y * PACKED + start : y * PACKED + stop, :].astype(jnp.float32)

    def put(i, j, tile):
        gram[i * TILE : (i + 1) * TILE, j * TILE : (j + 1) * TILE] = tile.astype(gram.dtype)

    def put_both(i, j, tile):
        put(i, j, tile)
        put(j, i, tile.T)

    for y in range(GROUPS):
        put_both(y, (y + 1) % 4, part(y, 0, 128))
        put_both(4, y, jnp.concatenate([part(y, 192, 256), zeros], axis=0))
        upper, corner = part(y, 256, 320), part(y, 320, 384)
        mirrored = jnp.concatenate([upper, zeros], axis=0).T
        lower = jnp.where(left_half(HALF), mirrored[HALF:], corner)
        put(y, y, jnp.concatenate([upper, lower], axis=0))
        trace += jnp.where(row == col, upper, 0.0) + jnp.where(row + HALF == col, corner, 0.0)
        if y == 0:
            trace += jnp.where(row == col, corner, 0.0)
            last = jnp.where(left_half(HALF), corner, 0.0)
            put(4, 4, jnp.concatenate([last, zeros], axis=0))
    for i in range(2):
        put_both(i, i + 2, jnp.concatenate([part(i, 128, 192), part(i + 2, 128, 192)], axis=0))

    total = jnp.sum(trace, axis=(0, 1), keepdims=True)
    inv_norm = 1.0 / (jnp.sqrt(total) + norm_eps)
    inv_square = inv_norm * inv_norm

    def dot(a, b):
        return jnp.dot(a, b, preferred_element_type=jnp.float32)

    g = gram[...]
    square = dot(g, g) * inv_square
    poly[...] = (
        (cubic_coeff * g.astype(jnp.float32) + quintic_coeff * square) * inv_square
    ).astype(poly.dtype)
    half = (linear_coeff * g.astype(jnp.float32) + dot(g, poly[...])) * inv_square
    work[...] = half.astype(work.dtype)
    second = (linear_coeff * half + dot(poly[...], work[...])).astype(gram.dtype)

    rows = rows_ref[...]
    first = (linear_coeff * rows.astype(jnp.float32) + dot(rows, poly[...])) * inv_norm
    first = first.astype(jnp.bfloat16)

    gram[...] = second
    g = gram[...]
    work[...] = (
        cubic_coeff * g.astype(jnp.float32) + quintic_coeff * dot(g, g)
    ).astype(work.dtype)
    result = linear_coeff * first.astype(jnp.float32) + dot(first, work[...])
    out_ref[...] = (result * factor)[:, : out_ref.shape[1]].astype(out_ref.dtype)


VMEM = pl.BlockSpec(memory_space=pltpu.VMEM)
HBM = pl.BlockSpec(memory_space=pl.ANY)
PARAMS = pltpu.CompilerParams(vmem_limit_bytes=32 * 1024 * 1024)


def bf16(*shape):
    return jax.ShapeDtypeStruct(shape, jnp.bfloat16)


def gram(received, momentum):
    rows = momentum.shape[0]
    return pl.pallas_call(
        gram_kernel,
        out_shape=(
            bf16(rows, WIDE),
            bf16(GROUPS * PACKED, TILE),
            jax.ShapeDtypeStruct(momentum.shape, momentum.dtype),
        ),
        in_specs=[VMEM, HBM],
        out_specs=(VMEM, VMEM, HBM),
        scratch_shapes=[pltpu.VMEM(momentum.shape, momentum.dtype)] * 2
        + [pltpu.SemaphoreType.DMA] * 2,
        compiler_params=PARAMS,
    )(received, momentum)


def total_of(parts, receivers):
    return pl.pallas_call(
        sum_kernel,
        out_shape=bf16(receivers, *parts.shape[1:]),
        in_specs=[VMEM],
        out_specs=VMEM,
        compiler_params=PARAMS,
    )(parts)


def newton(factor, packed, wide, width):
    return pl.pallas_call(
        functools.partial(newton_kernel, factor),
        out_shape=bf16(wide.shape[0], width),
        in_specs=[VMEM, VMEM],
        out_specs=VMEM,
        scratch_shapes=[pltpu.VMEM((WIDE, WIDE), jnp.bfloat16)] * 3,
        compiler_params=PARAMS,
    )(packed, wide)


def local(partial_grads, momentum):
    rep, cluster = ("x", "core"), ("near", "y")
    blocks = lax.axis_size("block")
    members = lax.axis_size(cluster)
    row_count, kv_width = momentum.shape[1:]
    factor = 0.2 * math.sqrt(max(row_count * blocks * members, kv_width))

    received = lax.all_to_all(partial_grads[0], rep, 0, 0, tiled=True)
    wide, packed, new_momentum = gram(received, momentum[0])

    packed = packed.reshape(members, GROUPS * PACKED // members, TILE)
    packed = lax.all_to_all(packed, cluster, 0, 0, tiled=True)
    packed = lax.all_to_all(total_of(packed, blocks), "block", 0, 0, tiled=True)
    packed = lax.all_to_all(total_of(packed, members), cluster, 0, 0, tiled=True)
    packed = packed.reshape(GROUPS * PACKED, TILE)

    update = newton(factor, packed, wide, kv_width)
    update = lax.all_gather(update, rep, axis=0, tiled=False)
    return (update, new_momentum[None])


def solution(mesh):
    devices = np.asarray(mesh.devices)
    fine = Mesh(devices.reshape(4, 2, 4, 8, 4), ("x", "core", "block", "near", "y"))
    rep, shard = ("x", "core"), ("block", "near", "y")
    return jax.shard_map(
        local,
        mesh=fine,
        in_specs=(P(rep, None, shard, None), P(rep, shard, None)),
        out_specs=(P(None, shard, None), P(rep, shard, None)),
        check_vma=False,
    )
```

```python
import functools
import math

import jax
import jax.numpy as jnp
import numpy as np
from jax import lax
from jax.experimental import pallas as pl
from jax.experimental.pallas import tpu as pltpu
from jax.sharding import Mesh
from jax.sharding import PartitionSpec as P

linear_coeff = 3.4445
cubic_coeff = -4.775
quintic_coeff = 2.0315
momentum_rate = 0.9
norm_eps = 1e-06

TILE = 128
HALF = 64
TILES = 5
WIDE = TILE * TILES
GROUPS = 4
PACKED = 384


def left_half(rows):
    return lax.broadcasted_iota(jnp.int32, (rows, TILE), 1) < HALF


def gram_kernel(
    received_ref, momentum_ref, wide_ref, packed_ref, new_ref, momentum, new, read_done, write_done
):
    read = pltpu.make_async_copy(momentum_ref, momentum, read_done)
    read.start()
    summed = received_ref[0].astype(jnp.float32)
    for part in range(1, received_ref.shape[0]):
        summed += received_ref[part].astype(jnp.float32)
    read.wait()
    updated = momentum_rate * momentum[...] + summed
    new[...] = updated
    write = pltpu.make_async_copy(new, new_ref, write_done)
    write.start()
    velocity = (summed + momentum_rate * updated).astype(wide_ref.dtype)
    rows, width = velocity.shape
    padding = jnp.zeros((rows, WIDE - width), wide_ref.dtype)
    wide_ref[...] = jnp.concatenate([velocity, padding], axis=1)

    def tile(i, j):
        return lax.dot_general(
            wide_ref[:, i * TILE : (i + 1) * TILE],
            wide_ref[:, j * TILE : (j + 1) * TILE],
            (((0,), (0,)), ((), ())),
            preferred_element_type=jnp.float32,
        )

    def put(start, block):
        packed_ref[start : start + block.shape[0], :] = block.astype(packed_ref.dtype)

    last = tile(4, 4)[:HALF]
    for y in range(GROUPS):
        base = y * PACKED
        put(base, tile(y, (y + 1) % 4))
        put(base + 192, tile(4, y)[:HALF])
        diagonal = tile(y, y)
        put(base + 256, diagonal[:HALF])
        put(base + 320, jnp.where(left_half(HALF), last, diagonal[HALF:]))
    for i in range(2):
        split = tile(i, i + 2)
        put(i * PACKED + 128, split[:HALF])
        put((i + 2) * PACKED + 128, split[HALF:])
    write.wait()


def sum_kernel(parts_ref, out_ref):
    total = parts_ref[0].astype(jnp.float32)
    for part in range(1, parts_ref.shape[0]):
        total += parts_ref[part].astype(jnp.float32)
    rounded = total.astype(out_ref.dtype)
    for part in range(out_ref.shape[0]):
        out_ref[part] = rounded


def newton_kernel(factor, packed_ref, rows_ref, out_ref, gram, work, poly):
    zeros = jnp.zeros((HALF, TILE), jnp.float32)
    row = lax.broadcasted_iota(jnp.int32, (HALF, TILE), 0)
    col = lax.broadcasted_iota(jnp.int32, (HALF, TILE), 1)
    trace = zeros

    def part(y, start, stop):
        return packed_ref[y * PACKED + start : y * PACKED + stop, :].astype(jnp.float32)

    def put(i, j, tile):
        gram[i * TILE : (i + 1) * TILE, j * TILE : (j + 1) * TILE] = tile.astype(gram.dtype)

    def put_both(i, j, tile):
        put(i, j, tile)
        put(j, i, tile.T)

    for y in range(GROUPS):
        put_both(y, (y + 1) % 4, part(y, 0, 128))
        put_both(4, y, jnp.concatenate([part(y, 192, 256), zeros], axis=0))
        upper, corner = part(y, 256, 320), part(y, 320, 384)
        mirrored = jnp.concatenate([upper, zeros], axis=0).T
        lower = jnp.where(left_half(HALF), mirrored[HALF:], corner)
        put(y, y, jnp.concatenate([upper, lower], axis=0))
        trace += jnp.where(row == col, upper, 0.0) + jnp.where(row + HALF == col, corner, 0.0)
        if y == 0:
            trace += jnp.where(row == col, corner, 0.0)
            last = jnp.where(left_half(HALF), corner, 0.0)
            put(4, 4, jnp.concatenate([last, zeros], axis=0))
    for i in range(2):
        put_both(i, i + 2, jnp.concatenate([part(i, 128, 192), part(i + 2, 128, 192)], axis=0))

    total = jnp.sum(trace, axis=(0, 1), keepdims=True)
    inv_norm = 1.0 / (jnp.sqrt(total) + norm_eps)
    inv_square = inv_norm * inv_norm

    def dot(a, b):
        return jnp.dot(a, b, preferred_element_type=jnp.float32)

    columns = [slice(start, min(start + 2 * TILE, WIDE)) for start in range(0, WIDE, 2 * TILE)]
    rows = rows_ref[...]
    g = gram[...]
    for at in columns:
        scaled = (cubic_coeff * inv_square) * gram[:, at].astype(jnp.float32)
        square = (quintic_coeff * inv_square * inv_square) * dot(g, gram[:, at])
        poly[:, at] = (scaled + square).astype(poly.dtype)
    p = poly[...]
    for at in columns:
        scaled = (linear_coeff * inv_square) * gram[:, at].astype(jnp.float32)
        work[:, at] = (scaled + inv_square * dot(g, poly[:, at])).astype(work.dtype)
    first = ((linear_coeff * inv_norm) * rows.astype(jnp.float32) + inv_norm * dot(rows, p)).astype(
        jnp.bfloat16
    )
    for at in columns:
        half = linear_coeff * work[:, at].astype(jnp.float32)
        gram[:, at] = (half + dot(p, work[:, at])).astype(gram.dtype)
    g = gram[...]
    for at in columns:
        scaled = cubic_coeff * gram[:, at].astype(jnp.float32)
        work[:, at] = (scaled + quintic_coeff * dot(g, gram[:, at])).astype(work.dtype)
    result = (linear_coeff * factor) * first.astype(jnp.float32) + factor * dot(first, work[...])
    out_ref[...] = result[:, : out_ref.shape[1]].astype(out_ref.dtype)


VMEM = pl.BlockSpec(memory_space=pltpu.VMEM)
HBM = pl.BlockSpec(memory_space=pl.ANY)
PARAMS = pltpu.CompilerParams(vmem_limit_bytes=32 * 1024 * 1024)


def bf16(*shape):
    return jax.ShapeDtypeStruct(shape, jnp.bfloat16)


def gram(received, momentum):
    rows = momentum.shape[0]
    return pl.pallas_call(
        gram_kernel,
        out_shape=(
            bf16(rows, WIDE),
            bf16(GROUPS * PACKED, TILE),
            jax.ShapeDtypeStruct(momentum.shape, momentum.dtype),
        ),
        in_specs=[VMEM, HBM],
        out_specs=(VMEM, VMEM, HBM),
        scratch_shapes=[pltpu.VMEM(momentum.shape, momentum.dtype)] * 2
        + [pltpu.SemaphoreType.DMA] * 2,
        compiler_params=PARAMS,
    )(received, momentum)


def total_of(parts, receivers):
    return pl.pallas_call(
        sum_kernel,
        out_shape=bf16(receivers, *parts.shape[1:]),
        in_specs=[VMEM],
        out_specs=VMEM,
        compiler_params=PARAMS,
    )(parts)


def newton(factor, packed, wide, width):
    return pl.pallas_call(
        functools.partial(newton_kernel, factor),
        out_shape=bf16(wide.shape[0], width),
        in_specs=[VMEM, VMEM],
        out_specs=VMEM,
        scratch_shapes=[pltpu.VMEM((WIDE, WIDE), jnp.bfloat16)] * 3,
        compiler_params=PARAMS,
    )(packed, wide)


def local(partial_grads, momentum):
    rep, cluster = ("x", "core"), ("near", "y")
    pair, quads = lax.axis_size("pair"), lax.axis_size("quad")
    members = lax.axis_size(cluster)
    row_count, kv_width = momentum.shape[1:]
    factor = 0.2 * math.sqrt(max(row_count * pair * quads * members, kv_width))

    received = lax.all_to_all(partial_grads[0], rep, 0, 0, tiled=True)
    wide, packed, new_momentum = gram(received, momentum[0])

    packed = packed.reshape(members, GROUPS * PACKED // members, TILE)
    packed = lax.all_to_all(packed, cluster, 0, 0, tiled=True)
    packed = lax.all_to_all(total_of(packed, pair), "pair", 0, 0, tiled=True)
    packed = lax.all_to_all(total_of(packed, quads), "quad", 0, 0, tiled=True)
    packed = lax.all_to_all(total_of(packed, members), cluster, 0, 0, tiled=True)
    packed = packed.reshape(GROUPS * PACKED, TILE)

    update = newton(factor, packed, wide, kv_width)
    update = lax.all_gather(update, rep, axis=0, tiled=False)
    return (update, new_momentum[None])


def solution(mesh):
    devices = np.asarray(mesh.devices)
    fine = Mesh(devices.reshape(4, 2, 4, 2, 4, 4), ("x", "core", "quad", "pair", "near", "y"))
    rep, shard = ("x", "core"), ("quad", "pair", "near", "y")
    return jax.shard_map(
        local,
        mesh=fine,
        in_specs=(P(rep, None, shard, None), P(rep, shard, None)),
        out_specs=(P(None, shard, None), P(rep, shard, None)),
        check_vma=False,
    )
```

```python
import functools
import math

import jax
import jax.numpy as jnp
import numpy as np
from jax import lax
from jax.experimental import pallas as pl
from jax.experimental.pallas import tpu as pltpu
from jax.sharding import Mesh
from jax.sharding import PartitionSpec as P

linear_coeff = 3.4445
cubic_coeff = -4.775
quintic_coeff = 2.0315
momentum_rate = 0.9
norm_eps = 1e-06

TILE = 128
HALF = 64
TILES = 5
WIDE = TILE * TILES
GROUPS = 4
PACKED = 384


def left_half(rows):
    return lax.broadcasted_iota(jnp.int32, (rows, TILE), 1) < HALF


def gram_kernel(
    received_ref, momentum_ref, wide_ref, packed_ref, new_ref, momentum, new, read_done, write_done
):
    read = pltpu.make_async_copy(momentum_ref, momentum, read_done)
    read.start()
    summed = received_ref[0].astype(jnp.float32)
    for part in range(1, received_ref.shape[0]):
        summed += received_ref[part].astype(jnp.float32)
    read.wait()
    updated = momentum_rate * momentum[...] + summed
    new[...] = updated
    write = pltpu.make_async_copy(new, new_ref, write_done)
    write.start()
    velocity = (summed + momentum_rate * updated).astype(wide_ref.dtype)
    rows, width = velocity.shape
    padding = jnp.zeros((rows, WIDE - width), wide_ref.dtype)
    wide_ref[...] = jnp.concatenate([velocity, padding], axis=1)

    def tile(i, j):
        return lax.dot_general(
            wide_ref[:, i * TILE : (i + 1) * TILE],
            wide_ref[:, j * TILE : (j + 1) * TILE],
            (((0,), (0,)), ((), ())),
            preferred_element_type=jnp.float32,
        )

    def put(start, block):
        packed_ref[start : start + block.shape[0], :] = block.astype(packed_ref.dtype)

    last = tile(4, 4)[:HALF]
    for y in range(GROUPS):
        base = y * PACKED
        put(base, tile(y, (y + 1) % 4))
        put(base + 192, tile(4, y)[:HALF])
        diagonal = tile(y, y)
        put(base + 256, diagonal[:HALF])
        put(base + 320, jnp.where(left_half(HALF), last, diagonal[HALF:]))
    for i in range(2):
        split = tile(i, i + 2)
        put(i * PACKED + 128, split[:HALF])
        put((i + 2) * PACKED + 128, split[HALF:])
    write.wait()


def sum_kernel(parts_ref, out_ref):
    total = parts_ref[0].astype(jnp.float32)
    for part in range(1, parts_ref.shape[0]):
        total += parts_ref[part].astype(jnp.float32)
    rounded = total.astype(out_ref.dtype)
    for part in range(out_ref.shape[0]):
        out_ref[part] = rounded


def newton_kernel(factor, packed_ref, rows_ref, out_ref, gram, work, poly):
    zeros = jnp.zeros((HALF, TILE), jnp.float32)
    row = lax.broadcasted_iota(jnp.int32, (HALF, TILE), 0)
    col = lax.broadcasted_iota(jnp.int32, (HALF, TILE), 1)
    trace = zeros

    def part(y, start, stop):
        return packed_ref[y * PACKED + start : y * PACKED + stop, :].astype(jnp.float32)

    def put(i, j, tile):
        gram[i * TILE : (i + 1) * TILE, j * TILE : (j + 1) * TILE] = tile.astype(gram.dtype)

    def put_both(i, j, tile):
        put(i, j, tile)
        put(j, i, tile.T)

    for y in range(GROUPS):
        put_both(y, (y + 1) % 4, part(y, 0, 128))
        put_both(4, y, jnp.concatenate([part(y, 192, 256), zeros], axis=0))
        upper, corner = part(y, 256, 320), part(y, 320, 384)
        mirrored = jnp.concatenate([upper, zeros], axis=0).T
        lower = jnp.where(left_half(HALF), mirrored[HALF:], corner)
        put(y, y, jnp.concatenate([upper, lower], axis=0))
        trace += jnp.where(row == col, upper, 0.0) + jnp.where(row + HALF == col, corner, 0.0)
        if y == 0:
            trace += jnp.where(row == col, corner, 0.0)
            last = jnp.where(left_half(HALF), corner, 0.0)
            put(4, 4, jnp.concatenate([last, zeros], axis=0))
    for i in range(2):
        put_both(i, i + 2, jnp.concatenate([part(i, 128, 192), part(i + 2, 128, 192)], axis=0))

    total = jnp.sum(trace, axis=(0, 1), keepdims=True)
    inv_norm = 1.0 / (jnp.sqrt(total) + norm_eps)
    inv_square = inv_norm * inv_norm

    def dot(a, b):
        return jnp.dot(a, b, preferred_element_type=jnp.float32)

    edges = [(0, 2 * TILE), (2 * TILE, 4 * TILE), (4 * TILE, WIDE)]

    def symmetric(store, product):
        for start, stop in edges:
            to = min(stop, WIDE - HALF)
            block = product(slice(0, to), slice(start, stop))
            store[0:to, start:stop] = block.astype(store.dtype)
            if start:
                store[start:stop, 0:start] = block[:start].T.astype(store.dtype)

    rows = rows_ref[...]
    for store in (poly, work):
        store[WIDE - HALF :, WIDE - TILE :] = jnp.zeros((HALF, TILE), store.dtype)
    symmetric(
        poly,
        lambda to, at: (cubic_coeff * inv_square) * gram[to, at].astype(jnp.float32)
        + (quintic_coeff * inv_square * inv_square) * dot(gram[to, :], gram[:, at]),
    )
    symmetric(
        work,
        lambda to, at: (linear_coeff * inv_square) * gram[to, at].astype(jnp.float32)
        + inv_square * dot(gram[to, :], poly[:, at]),
    )
    first = (linear_coeff * inv_norm) * rows.astype(jnp.float32) + inv_norm * dot(rows, poly[...])
    first = first.astype(jnp.bfloat16)
    symmetric(
        gram,
        lambda to, at: linear_coeff * work[to, at].astype(jnp.float32)
        + dot(poly[to, :], work[:, at]),
    )
    symmetric(
        work,
        lambda to, at: cubic_coeff * gram[to, at].astype(jnp.float32)
        + quintic_coeff * dot(gram[to, :], gram[:, at]),
    )
    result = (linear_coeff * factor) * first.astype(jnp.float32) + factor * dot(first, work[...])
    update = result[:, : out_ref.shape[2]].astype(out_ref.dtype)
    for receiver in range(out_ref.shape[0]):
        out_ref[receiver] = update


VMEM = pl.BlockSpec(memory_space=pltpu.VMEM)
HBM = pl.BlockSpec(memory_space=pl.ANY)
PARAMS = pltpu.CompilerParams(vmem_limit_bytes=32 * 1024 * 1024)


def bf16(*shape):
    return jax.ShapeDtypeStruct(shape, jnp.bfloat16)


def gram(received, momentum):
    rows = momentum.shape[0]
    return pl.pallas_call(
        gram_kernel,
        out_shape=(
            bf16(rows, WIDE),
            bf16(GROUPS * PACKED, TILE),
            jax.ShapeDtypeStruct(momentum.shape, momentum.dtype),
        ),
        in_specs=[VMEM, HBM],
        out_specs=(VMEM, VMEM, HBM),
        scratch_shapes=[pltpu.VMEM(momentum.shape, momentum.dtype)] * 2
        + [pltpu.SemaphoreType.DMA] * 2,
        compiler_params=PARAMS,
    )(received, momentum)


def total_of(parts, receivers):
    return pl.pallas_call(
        sum_kernel,
        out_shape=bf16(receivers, *parts.shape[1:]),
        in_specs=[VMEM],
        out_specs=VMEM,
        compiler_params=PARAMS,
    )(parts)


def newton(factor, packed, wide, width, receivers):
    return pl.pallas_call(
        functools.partial(newton_kernel, factor),
        out_shape=bf16(receivers, wide.shape[0], width),
        in_specs=[VMEM, VMEM],
        out_specs=VMEM,
        scratch_shapes=[pltpu.VMEM((WIDE, WIDE), jnp.bfloat16)] * 3,
        compiler_params=PARAMS,
    )(packed, wide)


def local(partial_grads, momentum):
    rep, cluster = ("x", "core"), ("near", "y")
    pair, quads = lax.axis_size("pair"), lax.axis_size("quad")
    members = lax.axis_size(cluster)
    row_count, kv_width = momentum.shape[1:]
    factor = 0.2 * math.sqrt(max(row_count * pair * quads * members, kv_width))

    received = lax.all_to_all(partial_grads[0], rep, 0, 0, tiled=True)
    wide, packed, new_momentum = gram(received, momentum[0])

    packed = packed.reshape(members, GROUPS * PACKED // members, TILE)
    packed = lax.all_to_all(packed, cluster, 0, 0, tiled=True)
    packed = lax.all_to_all(total_of(packed, pair), "pair", 0, 0, tiled=True)
    packed = lax.all_to_all(total_of(packed, quads), "quad", 0, 0, tiled=True)
    packed = lax.all_to_all(total_of(packed, members), cluster, 0, 0, tiled=True)
    packed = packed.reshape(GROUPS * PACKED, TILE)

    update = newton(factor, packed, wide, kv_width, lax.axis_size("x"))
    update = lax.all_to_all(update, "x", 0, 0, tiled=True)
    update = lax.all_gather(update, "core", axis=1)
    return (update.reshape(-1, row_count, kv_width), new_momentum[None])


def solution(mesh):
    devices = np.asarray(mesh.devices)
    fine = Mesh(devices.reshape(4, 2, 4, 2, 4, 4), ("x", "core", "quad", "pair", "near", "y"))
    rep, shard = ("x", "core"), ("quad", "pair", "near", "y")
    return jax.shard_map(
        local,
        mesh=fine,
        in_specs=(P(rep, None, shard, None), P(rep, shard, None)),
        out_specs=(P(None, shard, None), P(rep, shard, None)),
        check_vma=False,
    )
```

```python
import functools
import math

import jax
import jax.numpy as jnp
import numpy as np
from jax import lax
from jax.experimental import pallas as pl
from jax.experimental.pallas import tpu as pltpu
from jax.sharding import Mesh
from jax.sharding import PartitionSpec as P

linear_coeff = 3.4445
cubic_coeff = -4.775
quintic_coeff = 2.0315
momentum_rate = 0.9
norm_eps = 1e-06

TILE = 128
HALF = 64
TILES = 5
WIDE = TILE * TILES
GROUPS = 4
PACKED = 384


def left_half(rows):
    return lax.broadcasted_iota(jnp.int32, (rows, TILE), 1) < HALF


def gram_kernel(
    received_ref, momentum_ref, wide_ref, packed_ref, new_ref, momentum, new, read_done, write_done
):
    read = pltpu.make_async_copy(momentum_ref, momentum, read_done)
    read.start()
    summed = received_ref[0].astype(jnp.float32)
    for part in range(1, received_ref.shape[0]):
        summed += received_ref[part].astype(jnp.float32)
    read.wait()
    updated = momentum_rate * momentum[...] + summed
    new[...] = updated
    write = pltpu.make_async_copy(new, new_ref, write_done)
    write.start()
    velocity = (summed + momentum_rate * updated).astype(wide_ref.dtype)
    rows, width = velocity.shape
    padding = jnp.zeros((rows, WIDE - width), wide_ref.dtype)
    wide_ref[...] = jnp.concatenate([velocity, padding], axis=1)

    def tile(i, j):
        return lax.dot_general(
            wide_ref[:, i * TILE : (i + 1) * TILE],
            wide_ref[:, j * TILE : (j + 1) * TILE],
            (((0,), (0,)), ((), ())),
            preferred_element_type=jnp.float32,
        )

    def put(start, block):
        packed_ref[start : start + block.shape[0], :] = block.astype(packed_ref.dtype)

    last = tile(4, 4)[:HALF]
    for y in range(GROUPS):
        base = y * PACKED
        put(base, tile(y, (y + 1) % 4))
        put(base + 192, tile(4, y)[:HALF])
        diagonal = tile(y, y)
        put(base + 256, diagonal[:HALF])
        put(base + 320, jnp.where(left_half(HALF), last, diagonal[HALF:]))
    for i in range(2):
        split = tile(i, i + 2)
        put(i * PACKED + 128, split[:HALF])
        put((i + 2) * PACKED + 128, split[HALF:])
    write.wait()


def sum_kernel(parts_ref, out_ref):
    total = parts_ref[0].astype(jnp.float32)
    for part in range(1, parts_ref.shape[0]):
        total += parts_ref[part].astype(jnp.float32)
    rounded = total.astype(out_ref.dtype)
    for part in range(out_ref.shape[0]):
        out_ref[part] = rounded


def newton_kernel(factor, packed_ref, rows_ref, out_ref, gram, work, poly):
    zeros = jnp.zeros((HALF, TILE), jnp.float32)
    row = lax.broadcasted_iota(jnp.int32, (HALF, TILE), 0)
    col = lax.broadcasted_iota(jnp.int32, (HALF, TILE), 1)
    trace = zeros

    def part(y, start, stop):
        return packed_ref[y * PACKED + start : y * PACKED + stop, :].astype(jnp.float32)

    def put(i, j, tile):
        gram[i * TILE : (i + 1) * TILE, j * TILE : (j + 1) * TILE] = tile.astype(gram.dtype)

    def put_both(i, j, tile):
        put(i, j, tile)
        put(j, i, tile.T)

    for y in range(GROUPS):
        put_both(y, (y + 1) % 4, part(y, 0, 128))
        put_both(4, y, jnp.concatenate([part(y, 192, 256), zeros], axis=0))
        upper, corner = part(y, 256, 320), part(y, 320, 384)
        mirrored = jnp.concatenate([upper, zeros], axis=0).T
        lower = jnp.where(left_half(HALF), mirrored[HALF:], corner)
        put(y, y, jnp.concatenate([upper, lower], axis=0))
        trace += jnp.where(row == col, upper, 0.0) + jnp.where(row + HALF == col, corner, 0.0)
        if y == 0:
            trace += jnp.where(row == col, corner, 0.0)
            last = jnp.where(left_half(HALF), corner, 0.0)
            put(4, 4, jnp.concatenate([last, zeros], axis=0))
    for i in range(2):
        put_both(i, i + 2, jnp.concatenate([part(i, 128, 192), part(i + 2, 128, 192)], axis=0))

    total = jnp.sum(trace, axis=(0, 1), keepdims=True)
    inv_norm = 1.0 / (jnp.sqrt(total) + norm_eps)
    inv_square = inv_norm * inv_norm

    def dot(a, b):
        return jnp.dot(a, b, preferred_element_type=jnp.float32)

    edges = [(0, 2 * TILE), (2 * TILE, 4 * TILE), (4 * TILE, WIDE)]

    def symmetric(store, product):
        for start, stop in edges:
            to = min(stop, WIDE - HALF)
            block = product(slice(0, to), slice(start, stop))
            store[0:to, start:stop] = block.astype(store.dtype)
            if start:
                store[start:stop, 0:start] = block[:start].T.astype(store.dtype)

    rows = rows_ref[...]
    for store in (poly, work):
        store[WIDE - HALF :, WIDE - TILE :] = jnp.zeros((HALF, TILE), store.dtype)
    symmetric(
        poly,
        lambda to, at: (cubic_coeff * inv_square) * gram[to, at].astype(jnp.float32)
        + (quintic_coeff * inv_square * inv_square) * dot(gram[to, :], gram[:, at]),
    )
    symmetric(
        work,
        lambda to, at: (linear_coeff * inv_square) * gram[to, at].astype(jnp.float32)
        + inv_square * dot(gram[to, :], poly[:, at]),
    )
    first = (linear_coeff * inv_norm) * rows.astype(jnp.float32) + inv_norm * dot(rows, poly[...])
    first = first.astype(jnp.bfloat16)
    symmetric(
        gram,
        lambda to, at: linear_coeff * work[to, at].astype(jnp.float32)
        + dot(poly[to, :], work[:, at]),
    )
    symmetric(
        work,
        lambda to, at: cubic_coeff * gram[to, at].astype(jnp.float32)
        + quintic_coeff * dot(gram[to, :], gram[:, at]),
    )
    result = (linear_coeff * factor) * first.astype(jnp.float32) + factor * dot(first, work[...])
    update = result[:, : out_ref.shape[2]].astype(out_ref.dtype)
    for receiver in range(out_ref.shape[0]):
        out_ref[receiver] = update


VMEM = pl.BlockSpec(memory_space=pltpu.VMEM)
HBM = pl.BlockSpec(memory_space=pl.ANY)
PARAMS = pltpu.CompilerParams(vmem_limit_bytes=32 * 1024 * 1024)


def bf16(*shape):
    return jax.ShapeDtypeStruct(shape, jnp.bfloat16)


def gram(received, momentum):
    rows = momentum.shape[0]
    return pl.pallas_call(
        gram_kernel,
        out_shape=(
            bf16(rows, WIDE),
            bf16(GROUPS * PACKED, TILE),
            jax.ShapeDtypeStruct(momentum.shape, momentum.dtype),
        ),
        in_specs=[VMEM, HBM],
        out_specs=(VMEM, VMEM, HBM),
        scratch_shapes=[pltpu.VMEM(momentum.shape, momentum.dtype)] * 2
        + [pltpu.SemaphoreType.DMA] * 2,
        compiler_params=PARAMS,
    )(received, momentum)


def total_of(parts, receivers):
    return pl.pallas_call(
        sum_kernel,
        out_shape=bf16(receivers, *parts.shape[1:]),
        in_specs=[VMEM],
        out_specs=VMEM,
        compiler_params=PARAMS,
    )(parts)


def newton(factor, packed, wide, width, receivers):
    return pl.pallas_call(
        functools.partial(newton_kernel, factor),
        out_shape=bf16(receivers, wide.shape[0], width),
        in_specs=[VMEM, VMEM],
        out_specs=VMEM,
        scratch_shapes=[pltpu.VMEM((WIDE, WIDE), jnp.bfloat16)] * 3,
        compiler_params=PARAMS,
    )(packed, wide)


def local(partial_grads, momentum):
    rep, cluster = ("x", "core"), ("near", "y")
    blocks = lax.axis_size("block")
    members = lax.axis_size(cluster)
    row_count, kv_width = momentum.shape[1:]
    factor = 0.2 * math.sqrt(max(row_count * blocks * members, kv_width))

    received = lax.all_to_all(partial_grads[0], rep, 0, 0, tiled=True)
    wide, packed, new_momentum = gram(received, momentum[0])

    packed = packed.reshape(members, GROUPS * PACKED // members, TILE)
    packed = lax.all_to_all(packed, cluster, 0, 0, tiled=True)
    packed = lax.all_to_all(total_of(packed, blocks), "block", 0, 0, tiled=True)
    packed = lax.all_to_all(total_of(packed, members), cluster, 0, 0, tiled=True)
    packed = packed.reshape(GROUPS * PACKED, TILE)

    update = newton(factor, packed, wide, kv_width, lax.axis_size("x"))
    update = lax.all_to_all(update, "x", 0, 0, tiled=True)
    update = lax.all_gather(update, "core", axis=1)
    return (update.reshape(-1, row_count, kv_width), new_momentum[None])


def solution(mesh):
    devices = np.asarray(mesh.devices)
    fine = Mesh(devices.reshape(4, 2, 8, 4, 4), ("x", "core", "block", "near", "y"))
    rep, shard = ("x", "core"), ("block", "near", "y")
    return jax.shard_map(
        local,
        mesh=fine,
        in_specs=(P(rep, None, shard, None), P(rep, shard, None)),
        out_specs=(P(None, shard, None), P(rep, shard, None)),
        check_vma=False,
    )
```

```python
import functools
import math

import jax
import jax.numpy as jnp
import numpy as np
from jax import lax
from jax.experimental import pallas as pl
from jax.experimental.pallas import tpu as pltpu
from jax.sharding import Mesh
from jax.sharding import PartitionSpec as P

linear_coeff = 3.4445
cubic_coeff = -4.775
quintic_coeff = 2.0315
momentum_rate = 0.9
norm_eps = 1e-06

TILE = 128
HALF = 64
TILES = 5
WIDE = TILE * TILES
GROUPS = 4
ACROSS, BELOW, DIAGONAL, CORNER, PACKED = 512, 768, 1024, 1280, 1408


def places(rows):
    return (lax.broadcasted_iota(jnp.int32, (rows, TILE), axis) for axis in range(2))


def gram_kernel(
    received_ref, momentum_ref, wide_ref, packed_ref, new_ref, momentum, new, read_done, write_done
):
    read = pltpu.make_async_copy(momentum_ref, momentum, read_done)
    read.start()
    summed = received_ref[0].astype(jnp.float32)
    for part in range(1, received_ref.shape[0]):
        summed += received_ref[part].astype(jnp.float32)
    read.wait()
    updated = momentum_rate * momentum[...] + summed
    new[...] = updated
    write = pltpu.make_async_copy(new, new_ref, write_done)
    write.start()
    velocity = (summed + momentum_rate * updated).astype(wide_ref.dtype)
    rows, width = velocity.shape
    padding = jnp.zeros((rows, WIDE - width), wide_ref.dtype)
    wide_ref[...] = jnp.concatenate([velocity, padding], axis=1)

    def tile(i, j):
        return lax.dot_general(
            wide_ref[:, i * TILE : (i + 1) * TILE],
            wide_ref[:, j * TILE : (j + 1) * TILE],
            (((0,), (0,)), ((), ())),
            preferred_element_type=jnp.float32,
        )

    def put(start, block):
        packed_ref[start : start + block.shape[0], :] = block.astype(packed_ref.dtype)

    row, col = places(HALF)
    corner = tile(4, 4)[:HALF]
    for y in range(GROUPS):
        put(y * TILE, tile(y, (y + 1) % 4))
        put(BELOW + y * HALF, tile(4, y)[:HALF])
        square = tile(y, y)
        upper, lower = square[:HALF], square[HALF:]
        moved = jnp.concatenate([lower[:, HALF:], lower[:, :HALF]], axis=1)
        put(DIAGONAL + y * HALF, jnp.where(row > col, moved, upper))
        line = jnp.sum(jnp.where(row == col, moved, 0.0), axis=1, keepdims=True)
        corner = jnp.where(col == HALF + y, line, corner)
    for i in range(2):
        put(ACROSS + i * TILE, tile(i, i + 2))
    put(CORNER, corner)
    put(CORNER + HALF, jnp.zeros((HALF, TILE), jnp.float32))
    write.wait()


def sum_kernel(parts_ref, out_ref):
    total = parts_ref[0].astype(jnp.float32)
    for part in range(1, parts_ref.shape[0]):
        total += parts_ref[part].astype(jnp.float32)
    rounded = total.astype(out_ref.dtype)
    for part in range(out_ref.shape[0]):
        out_ref[part] = rounded


def newton_kernel(factor, packed_ref, rows_ref, out_ref, gram, work, poly):
    zeros = jnp.zeros((HALF, TILE), jnp.float32)
    row, col = places(HALF)

    def part(start, rows):
        return packed_ref[start : start + rows, :].astype(jnp.float32)

    def put(i, j, tile):
        gram[i * TILE : (i + 1) * TILE, j * TILE : (j + 1) * TILE] = tile.astype(gram.dtype)

    def put_both(i, j, tile):
        put(i, j, tile)
        put(j, i, tile.T)

    corner = part(CORNER, HALF)
    block = jnp.where(col < HALF, corner, 0.0)
    put(4, 4, jnp.concatenate([block, zeros], axis=0))
    trace = jnp.where(row == col, block, 0.0)
    for y in range(GROUPS):
        put_both(y, (y + 1) % 4, part(y * TILE, TILE))
        put_both(4, y, jnp.concatenate([part(BELOW + y * HALF, HALF), zeros], axis=0))
        square = part(DIAGONAL + y * HALF, HALF)
        turned = jnp.concatenate([square, zeros], axis=0).T
        line = jnp.where(col == HALF + y, corner, 0.0)
        trace += jnp.where(row == col, square, 0.0) + line
        line = jnp.sum(line, axis=1, keepdims=True)
        upper = jnp.where(row > col, turned[:HALF], square)
        lower = jnp.where(row > col, square, jnp.where(row < col, turned[:HALF], line))
        lower = jnp.concatenate([turned[HALF:, :HALF], lower[:, :HALF]], axis=1)
        put(y, y, jnp.concatenate([upper, lower], axis=0))
    for i in range(2):
        put_both(i, i + 2, part(ACROSS + i * TILE, TILE))

    total = jnp.sum(trace, axis=(0, 1), keepdims=True)
    inv_norm = 1.0 / (jnp.sqrt(total) + norm_eps)
    inv_square = inv_norm * inv_norm

    def dot(a, b):
        return jnp.dot(a, b, preferred_element_type=jnp.float32)

    edges = [(0, 2 * TILE), (2 * TILE, 4 * TILE), (4 * TILE, WIDE)]

    def symmetric(store, product):
        for start, stop in edges:
            to = min(stop, WIDE - HALF)
            block = product(slice(0, to), slice(start, stop))
            store[0:to, start:stop] = block.astype(store.dtype)
            if start:
                store[start:stop, 0:start] = block[:start].T.astype(store.dtype)

    rows = rows_ref[...]
    for store in (poly, work):
        store[WIDE - HALF :, WIDE - TILE :] = jnp.zeros((HALF, TILE), store.dtype)
    symmetric(
        poly,
        lambda to, at: (cubic_coeff * inv_square) * gram[to, at].astype(jnp.float32)
        + (quintic_coeff * inv_square * inv_square) * dot(gram[to, :], gram[:, at]),
    )
    symmetric(
        work,
        lambda to, at: (linear_coeff * inv_square) * gram[to, at].astype(jnp.float32)
        + inv_square * dot(gram[to, :], poly[:, at]),
    )
    first = (linear_coeff * inv_norm) * rows.astype(jnp.float32) + inv_norm * dot(rows, poly[...])
    first = first.astype(jnp.bfloat16)
    symmetric(
        gram,
        lambda to, at: linear_coeff * work[to, at].astype(jnp.float32)
        + dot(poly[to, :], work[:, at]),
    )
    symmetric(
        work,
        lambda to, at: cubic_coeff * gram[to, at].astype(jnp.float32)
        + quintic_coeff * dot(gram[to, :], gram[:, at]),
    )
    result = (linear_coeff * factor) * first.astype(jnp.float32) + factor * dot(first, work[...])
    update = result[:, : out_ref.shape[2]].astype(out_ref.dtype)
    for receiver in range(out_ref.shape[0]):
        out_ref[receiver] = update


VMEM = pl.BlockSpec(memory_space=pltpu.VMEM)
HBM = pl.BlockSpec(memory_space=pl.ANY)
PARAMS = pltpu.CompilerParams(vmem_limit_bytes=32 * 1024 * 1024)


def bf16(*shape):
    return jax.ShapeDtypeStruct(shape, jnp.bfloat16)


def gram(received, momentum):
    rows = momentum.shape[0]
    return pl.pallas_call(
        gram_kernel,
        out_shape=(
            bf16(rows, WIDE),
            bf16(PACKED, TILE),
            jax.ShapeDtypeStruct(momentum.shape, momentum.dtype),
        ),
        in_specs=[VMEM, HBM],
        out_specs=(VMEM, VMEM, HBM),
        scratch_shapes=[pltpu.VMEM(momentum.shape, momentum.dtype)] * 2
        + [pltpu.SemaphoreType.DMA] * 2,
        compiler_params=PARAMS,
    )(received, momentum)


def total_of(parts, receivers):
    return pl.pallas_call(
        sum_kernel,
        out_shape=bf16(receivers, *parts.shape[1:]),
        in_specs=[VMEM],
        out_specs=VMEM,
        compiler_params=PARAMS,
    )(parts)


def newton(factor, packed, wide, width, receivers):
    return pl.pallas_call(
        functools.partial(newton_kernel, factor),
        out_shape=bf16(receivers, wide.shape[0], width),
        in_specs=[VMEM, VMEM],
        out_specs=VMEM,
        scratch_shapes=[pltpu.VMEM((WIDE, WIDE), jnp.bfloat16)] * 3,
        compiler_params=PARAMS,
    )(packed, wide)


def local(partial_grads, momentum):
    rep, cluster = ("x", "core"), ("near", "y")
    blocks = lax.axis_size("block")
    members = lax.axis_size(cluster)
    row_count, kv_width = momentum.shape[1:]
    factor = 0.2 * math.sqrt(max(row_count * blocks * members, kv_width))

    received = lax.all_to_all(partial_grads[0], rep, 0, 0, tiled=True)
    wide, packed, new_momentum = gram(received, momentum[0])

    packed = packed.reshape(members, PACKED // members, TILE)
    packed = lax.all_to_all(packed, cluster, 0, 0, tiled=True)
    packed = lax.all_to_all(total_of(packed, blocks), "block", 0, 0, tiled=True)
    packed = lax.all_to_all(total_of(packed, members), cluster, 0, 0, tiled=True)
    packed = packed.reshape(PACKED, TILE)

    update = newton(factor, packed, wide, kv_width, lax.axis_size("x"))
    update = lax.all_to_all(update, "x", 0, 0, tiled=True)
    update = lax.all_gather(update, "core", axis=1)
    return (update.reshape(-1, row_count, kv_width), new_momentum[None])


def solution(mesh):
    devices = np.asarray(mesh.devices)
    fine = Mesh(devices.reshape(4, 2, 8, 4, 4), ("x", "core", "block", "near", "y"))
    rep, shard = ("x", "core"), ("block", "near", "y")
    return jax.shard_map(
        local,
        mesh=fine,
        in_specs=(P(rep, None, shard, None), P(rep, shard, None)),
        out_specs=(P(None, shard, None), P(rep, shard, None)),
        check_vma=False,
    )
```

```python
import functools
import math

import jax
import jax.numpy as jnp
import numpy as np
from jax import lax
from jax.experimental import pallas as pl
from jax.experimental.pallas import tpu as pltpu
from jax.sharding import Mesh
from jax.sharding import PartitionSpec as P

linear_coeff = 3.4445
cubic_coeff = -4.775
quintic_coeff = 2.0315
momentum_rate = 0.9
norm_eps = 1e-06

TILE = 128
HALF = 64
TILES = 5
WIDE = TILE * TILES
GROUPS = 4
ACROSS, BELOW, DIAGONAL, CORNER, PACKED = 512, 768, 1024, 1280, 1408


def places(rows):
    return (lax.broadcasted_iota(jnp.int32, (rows, TILE), axis) for axis in range(2))


def gram_kernel(
    received_ref, momentum_ref, wide_ref, packed_ref, new_ref, momentum, new, read_done, write_done
):
    read = pltpu.make_async_copy(momentum_ref, momentum, read_done)
    read.start()
    summed = received_ref[0].astype(jnp.float32)
    for part in range(1, received_ref.shape[0]):
        summed += received_ref[part].astype(jnp.float32)
    read.wait()
    updated = momentum_rate * momentum[...] + summed
    new[...] = updated
    write = pltpu.make_async_copy(new, new_ref, write_done)
    write.start()
    velocity = (summed + momentum_rate * updated).astype(wide_ref.dtype)
    rows, width = velocity.shape
    padding = jnp.zeros((rows, WIDE - width), wide_ref.dtype)
    wide_ref[...] = jnp.concatenate([velocity, padding], axis=1)

    def tile(i, j):
        return lax.dot_general(
            wide_ref[:, i * TILE : (i + 1) * TILE],
            wide_ref[:, j * TILE : (j + 1) * TILE],
            (((0,), (0,)), ((), ())),
            preferred_element_type=jnp.float32,
        )

    def put(start, block):
        packed_ref[start : start + block.shape[0], :] = block.astype(packed_ref.dtype)

    row, col = places(HALF)
    corner = tile(4, 4)[:HALF]
    for y in range(GROUPS):
        put(y * TILE, tile(y, (y + 1) % 4))
        put(BELOW + y * HALF, tile(4, y)[:HALF])
        square = tile(y, y)
        upper, lower = square[:HALF], square[HALF:]
        moved = jnp.concatenate([lower[:, HALF:], lower[:, :HALF]], axis=1)
        put(DIAGONAL + y * HALF, jnp.where(row > col, moved, upper))
        line = jnp.sum(jnp.where(row == col, moved, 0.0), axis=1, keepdims=True)
        corner = jnp.where(col == HALF + y, line, corner)
    for i in range(2):
        put(ACROSS + i * TILE, tile(i, i + 2))
    put(CORNER, corner)
    put(CORNER + HALF, jnp.zeros((HALF, TILE), jnp.float32))
    write.wait()


def sum_kernel(parts_ref, out_ref):
    total = parts_ref[0].astype(jnp.float32)
    for part in range(1, parts_ref.shape[0]):
        total += parts_ref[part].astype(jnp.float32)
    rounded = total.astype(out_ref.dtype)
    for part in range(out_ref.shape[0]):
        out_ref[part] = rounded


def newton_kernel(factor, packed_ref, rows_ref, out_ref, gram, work, poly):
    zeros = jnp.zeros((HALF, TILE), jnp.float32)
    row, col = places(HALF)

    def part(start, rows):
        return packed_ref[start : start + rows, :].astype(jnp.float32)

    def put(i, j, tile):
        gram[i * TILE : (i + 1) * TILE, j * TILE : (j + 1) * TILE] = tile.astype(gram.dtype)

    def put_both(i, j, tile):
        put(i, j, tile)
        put(j, i, tile.astype(gram.dtype).T)

    corner = part(CORNER, HALF)
    block = jnp.where(col < HALF, corner, 0.0)
    put(4, 4, jnp.concatenate([block, zeros], axis=0))
    trace = jnp.where(row == col, block, 0.0)
    for y in range(GROUPS):
        put_both(y, (y + 1) % 4, part(y * TILE, TILE))
        put_both(4, y, jnp.concatenate([part(BELOW + y * HALF, HALF), zeros], axis=0))
        square = part(DIAGONAL + y * HALF, HALF)
        turned = jnp.concatenate([square, zeros], axis=0).T
        line = jnp.where(col == HALF + y, corner, 0.0)
        trace += jnp.where(row == col, square, 0.0) + line
        line = jnp.sum(line, axis=1, keepdims=True)
        upper = jnp.where(row > col, turned[:HALF], square)
        lower = jnp.where(row > col, square, jnp.where(row < col, turned[:HALF], line))
        lower = jnp.concatenate([turned[HALF:, :HALF], lower[:, :HALF]], axis=1)
        put(y, y, jnp.concatenate([upper, lower], axis=0))
    for i in range(2):
        put_both(i, i + 2, part(ACROSS + i * TILE, TILE))

    total = jnp.sum(trace, axis=(0, 1), keepdims=True)
    inv_norm = 1.0 / (jnp.sqrt(total) + norm_eps)
    inv_square = inv_norm * inv_norm

    def dot(a, b):
        return jnp.dot(a, b, preferred_element_type=jnp.float32)

    edges = [(0, 2 * TILE), (2 * TILE, 4 * TILE), (4 * TILE, WIDE)]

    def symmetric(store, product):
        for start, stop in edges:
            to = min(stop, WIDE - HALF)
            block = product(slice(0, to), slice(start, stop))
            store[0:to, start:stop] = block.astype(store.dtype)
            if start:
                store[start:stop, 0:start] = block[:start].astype(store.dtype).T

    rows = rows_ref[...]
    for store in (poly, work):
        store[WIDE - HALF :, WIDE - TILE :] = jnp.zeros((HALF, TILE), store.dtype)
    symmetric(
        poly,
        lambda to, at: (cubic_coeff * inv_square) * gram[to, at].astype(jnp.float32)
        + (quintic_coeff * inv_square * inv_square) * dot(gram[to, :], gram[:, at]),
    )
    symmetric(
        work,
        lambda to, at: (linear_coeff * inv_square) * gram[to, at].astype(jnp.float32)
        + inv_square * dot(gram[to, :], poly[:, at]),
    )
    first = (linear_coeff * inv_norm) * rows.astype(jnp.float32) + inv_norm * dot(rows, poly[...])
    first = first.astype(jnp.bfloat16)
    symmetric(
        gram,
        lambda to, at: linear_coeff * work[to, at].astype(jnp.float32)
        + dot(poly[to, :], work[:, at]),
    )
    symmetric(
        work,
        lambda to, at: cubic_coeff * gram[to, at].astype(jnp.float32)
        + quintic_coeff * dot(gram[to, :], gram[:, at]),
    )
    result = (linear_coeff * factor) * first.astype(jnp.float32) + factor * dot(first, work[...])
    update = result[:, : out_ref.shape[2]].astype(out_ref.dtype)
    for receiver in range(out_ref.shape[0]):
        out_ref[receiver] = update


VMEM = pl.BlockSpec(memory_space=pltpu.VMEM)
HBM = pl.BlockSpec(memory_space=pl.ANY)
PARAMS = pltpu.CompilerParams(vmem_limit_bytes=32 * 1024 * 1024)


def bf16(*shape):
    return jax.ShapeDtypeStruct(shape, jnp.bfloat16)


def gram(received, momentum):
    rows = momentum.shape[0]
    return pl.pallas_call(
        gram_kernel,
        out_shape=(
            bf16(rows, WIDE),
            bf16(PACKED, TILE),
            jax.ShapeDtypeStruct(momentum.shape, momentum.dtype),
        ),
        in_specs=[VMEM, HBM],
        out_specs=(VMEM, VMEM, HBM),
        scratch_shapes=[pltpu.VMEM(momentum.shape, momentum.dtype)] * 2
        + [pltpu.SemaphoreType.DMA] * 2,
        compiler_params=PARAMS,
    )(received, momentum)


def total_of(parts, receivers):
    return pl.pallas_call(
        sum_kernel,
        out_shape=bf16(receivers, *parts.shape[1:]),
        in_specs=[VMEM],
        out_specs=VMEM,
        compiler_params=PARAMS,
    )(parts)


def newton(factor, packed, wide, width, receivers):
    return pl.pallas_call(
        functools.partial(newton_kernel, factor),
        out_shape=bf16(receivers, wide.shape[0], width),
        in_specs=[VMEM, VMEM],
        out_specs=VMEM,
        scratch_shapes=[pltpu.VMEM((WIDE, WIDE), jnp.bfloat16)] * 3,
        compiler_params=PARAMS,
    )(packed, wide)


def exchange(parts, axis, order):
    return lax.all_to_all(parts, axis, 0, 0, axis_index_groups=[order], tiled=True)


def local(partial_grads, momentum):
    rep, cluster = ("x", "core"), ("near", "y")
    blocks = lax.axis_size("block")
    members = lax.axis_size(cluster)
    lanes = lax.axis_size("y")
    cluster_order = [z * lanes + y for y in range(lanes) for z in range(members // lanes)]
    block_order = [*range(0, blocks, 2), *range(1, blocks, 2)]
    row_count, kv_width = momentum.shape[1:]
    factor = 0.2 * math.sqrt(max(row_count * blocks * members, kv_width))

    received = lax.all_to_all(partial_grads[0], rep, 0, 0, tiled=True)
    wide, packed, new_momentum = gram(received, momentum[0])

    packed = packed.reshape(members, PACKED // members, TILE)
    packed = exchange(packed, cluster, cluster_order)
    packed = exchange(total_of(packed, blocks), "block", block_order)
    packed = exchange(total_of(packed, members), cluster, cluster_order)
    packed = packed.reshape(PACKED, TILE)

    update = newton(factor, packed, wide, kv_width, lax.axis_size("x"))
    update = lax.all_to_all(update, "x", 0, 0, tiled=True)
    update = lax.all_gather(update, "core", axis=1)
    return (update.reshape(-1, row_count, kv_width), new_momentum[None])


def solution(mesh):
    devices = np.asarray(mesh.devices)
    fine = Mesh(devices.reshape(4, 2, 8, 4, 4), ("x", "core", "block", "near", "y"))
    rep, shard = ("x", "core"), ("block", "near", "y")
    return jax.shard_map(
        local,
        mesh=fine,
        in_specs=(P(rep, None, shard, None), P(rep, shard, None)),
        out_specs=(P(None, shard, None), P(rep, shard, None)),
        check_vma=False,
    )
```

```python
import functools
import math

import jax
import jax.numpy as jnp
import numpy as np
from jax import lax
from jax.experimental import pallas as pl
from jax.experimental.pallas import tpu as pltpu
from jax.sharding import Mesh
from jax.sharding import PartitionSpec as P

linear_coeff = 3.4445
cubic_coeff = -4.775
quintic_coeff = 2.0315
momentum_rate = 0.9
norm_eps = 1e-06

TILE = 128
HALF = 64
TILES = 5
WIDE = TILE * TILES
GROUPS = 4
ACROSS, BELOW, DIAGONAL, CORNER, PACKED = 512, 768, 1024, 1280, 1408


def places(rows):
    return (lax.broadcasted_iota(jnp.int32, (rows, TILE), axis) for axis in range(2))


def gram_kernel(
    received_ref, momentum_ref, wide_ref, packed_ref, new_ref, momentum, new, read_done, write_done
):
    read = pltpu.make_async_copy(momentum_ref, momentum, read_done)
    read.start()
    summed = received_ref[0].astype(jnp.float32)
    for part in range(1, received_ref.shape[0]):
        summed += received_ref[part].astype(jnp.float32)
    read.wait()
    updated = momentum_rate * momentum[...] + summed
    new[...] = updated
    write = pltpu.make_async_copy(new, new_ref, write_done)
    write.start()
    velocity = (summed + momentum_rate * updated).astype(wide_ref.dtype)
    rows, width = velocity.shape
    padding = jnp.zeros((rows, WIDE - width), wide_ref.dtype)
    wide_ref[...] = jnp.concatenate([velocity, padding], axis=1)

    def tile(i, j):
        return lax.dot_general(
            wide_ref[:, i * TILE : (i + 1) * TILE],
            wide_ref[:, j * TILE : (j + 1) * TILE],
            (((0,), (0,)), ((), ())),
            preferred_element_type=jnp.float32,
        )

    def put(start, block):
        packed_ref[start : start + block.shape[0], :] = block.astype(packed_ref.dtype)

    row, col = places(HALF)
    corner = tile(4, 4)[:HALF]
    for y in range(GROUPS):
        put(y * TILE, tile(y, (y + 1) % 4))
        put(BELOW + y * HALF, tile(4, y)[:HALF])
        square = tile(y, y)
        upper, lower = square[:HALF], square[HALF:]
        moved = jnp.concatenate([lower[:, HALF:], lower[:, :HALF]], axis=1)
        put(DIAGONAL + y * HALF, jnp.where(row > col, moved, upper))
        line = jnp.sum(jnp.where(row == col, moved, 0.0), axis=1, keepdims=True)
        corner = jnp.where(col == HALF + y, line, corner)
    for i in range(2):
        put(ACROSS + i * TILE, tile(i, i + 2))
    put(CORNER, corner)
    put(CORNER + HALF, jnp.zeros((HALF, TILE), jnp.float32))
    write.wait()


def sum_kernel(parts_ref, out_ref):
    total = parts_ref[0].astype(jnp.float32)
    for part in range(1, parts_ref.shape[0]):
        total += parts_ref[part].astype(jnp.float32)
    rounded = total.astype(out_ref.dtype)
    for part in range(out_ref.shape[0]):
        out_ref[part] = rounded


def newton_kernel(factor, packed_ref, rows_ref, out_ref, gram, work, poly):
    zeros = jnp.zeros((HALF, TILE), jnp.float32)
    row, col = places(HALF)

    def part(start, rows):
        return packed_ref[start : start + rows, :].astype(jnp.float32)

    def put(i, j, tile):
        gram[i * TILE : (i + 1) * TILE, j * TILE : (j + 1) * TILE] = tile.astype(gram.dtype)

    def put_both(i, j, tile):
        put(i, j, tile)
        put(j, i, tile.astype(gram.dtype).T)

    corner = part(CORNER, HALF)
    block = jnp.where(col < HALF, corner, 0.0)
    put(4, 4, jnp.concatenate([block, zeros], axis=0))
    trace = jnp.where(row == col, block, 0.0)
    for y in range(GROUPS):
        put_both(y, (y + 1) % 4, part(y * TILE, TILE))
        put_both(4, y, jnp.concatenate([part(BELOW + y * HALF, HALF), zeros], axis=0))
        square = part(DIAGONAL + y * HALF, HALF)
        turned = jnp.concatenate([square, zeros], axis=0).T
        line = jnp.where(col == HALF + y, corner, 0.0)
        trace += jnp.where(row == col, square, 0.0) + line
        line = jnp.sum(line, axis=1, keepdims=True)
        upper = jnp.where(row > col, turned[:HALF], square)
        lower = jnp.where(row > col, square, jnp.where(row < col, turned[:HALF], line))
        lower = jnp.concatenate([turned[HALF:, :HALF], lower[:, :HALF]], axis=1)
        put(y, y, jnp.concatenate([upper, lower], axis=0))
    for i in range(2):
        put_both(i, i + 2, part(ACROSS + i * TILE, TILE))

    total = jnp.sum(trace, axis=(0, 1), keepdims=True)
    inv_norm = 1.0 / (jnp.sqrt(total) + norm_eps)
    inv_square = inv_norm * inv_norm

    def dot(a, b):
        return jnp.dot(a, b, preferred_element_type=jnp.float32)

    edges = [(0, 2 * TILE), (2 * TILE, 4 * TILE), (4 * TILE, WIDE)]

    def symmetric(store, product):
        for start, stop in edges:
            to = min(stop, WIDE - HALF)
            block = product(slice(0, to), slice(start, stop))
            store[0:to, start:stop] = block.astype(store.dtype)
            if start:
                store[start:stop, 0:start] = block[:start].astype(store.dtype).T

    rows = rows_ref[...]
    for store in (poly, work):
        store[WIDE - HALF :, WIDE - TILE :] = jnp.zeros((HALF, TILE), store.dtype)
    symmetric(
        poly,
        lambda to, at: (cubic_coeff * inv_square) * gram[to, at].astype(jnp.float32)
        + (quintic_coeff * inv_square * inv_square) * dot(gram[to, :], gram[:, at]),
    )
    symmetric(
        work,
        lambda to, at: (linear_coeff * inv_square) * gram[to, at].astype(jnp.float32)
        + inv_square * dot(gram[to, :], poly[:, at]),
    )
    first = (linear_coeff * inv_norm) * rows.astype(jnp.float32) + inv_norm * dot(rows, poly[...])
    first = first.astype(jnp.bfloat16)
    symmetric(
        gram,
        lambda to, at: linear_coeff * work[to, at].astype(jnp.float32)
        + dot(poly[to, :], work[:, at]),
    )
    symmetric(
        work,
        lambda to, at: cubic_coeff * gram[to, at].astype(jnp.float32)
        + quintic_coeff * dot(gram[to, :], gram[:, at]),
    )
    result = (linear_coeff * factor) * first.astype(jnp.float32) + factor * dot(first, work[...])
    update = result[:, : out_ref.shape[2]].astype(out_ref.dtype)
    for receiver in range(out_ref.shape[0]):
        out_ref[receiver] = update


VMEM = pl.BlockSpec(memory_space=pltpu.VMEM)
HBM = pl.BlockSpec(memory_space=pl.ANY)
PARAMS = pltpu.CompilerParams(vmem_limit_bytes=32 * 1024 * 1024)


def bf16(*shape):
    return jax.ShapeDtypeStruct(shape, jnp.bfloat16)


def gram(received, momentum):
    rows = momentum.shape[0]
    return pl.pallas_call(
        gram_kernel,
        out_shape=(
            bf16(rows, WIDE),
            bf16(PACKED, TILE),
            jax.ShapeDtypeStruct(momentum.shape, momentum.dtype),
        ),
        in_specs=[VMEM, HBM],
        out_specs=(VMEM, VMEM, HBM),
        scratch_shapes=[pltpu.VMEM(momentum.shape, momentum.dtype)] * 2
        + [pltpu.SemaphoreType.DMA] * 2,
        compiler_params=PARAMS,
    )(received, momentum)


def total_of(parts, receivers):
    return pl.pallas_call(
        sum_kernel,
        out_shape=bf16(receivers, *parts.shape[1:]),
        in_specs=[VMEM],
        out_specs=VMEM,
        compiler_params=PARAMS,
    )(parts)


def newton(factor, packed, wide, width, receivers):
    return pl.pallas_call(
        functools.partial(newton_kernel, factor),
        out_shape=bf16(receivers, wide.shape[0], width),
        in_specs=[VMEM, VMEM],
        out_specs=VMEM,
        scratch_shapes=[pltpu.VMEM((WIDE, WIDE), jnp.bfloat16)] * 3,
        compiler_params=PARAMS,
    )(packed, wide)


def local(partial_grads, momentum):
    rep, cluster = ("x", "core"), ("near", "y")
    blocks = lax.axis_size("block")
    members = lax.axis_size(cluster)
    block_order = [*range(0, blocks, 2), *range(1, blocks, 2)]
    row_count, kv_width = momentum.shape[1:]
    factor = 0.2 * math.sqrt(max(row_count * blocks * members, kv_width))

    received = lax.all_to_all(partial_grads[0], rep, 0, 0, tiled=True)
    wide, packed, new_momentum = gram(received, momentum[0])

    packed = packed.reshape(members, PACKED // members, TILE)
    packed = lax.all_to_all(packed, cluster, 0, 0, tiled=True)
    packed = lax.all_to_all(
        total_of(packed, blocks), "block", 0, 0, axis_index_groups=[block_order], tiled=True
    )
    packed = lax.all_to_all(total_of(packed, members), cluster, 0, 0, tiled=True)
    packed = packed.reshape(PACKED, TILE)

    update = newton(factor, packed, wide, kv_width, lax.axis_size("x"))
    update = lax.all_to_all(update, "x", 0, 0, tiled=True)
    update = lax.all_gather(update, "core", axis=1)
    return (update.reshape(-1, row_count, kv_width), new_momentum[None])


def solution(mesh):
    devices = np.asarray(mesh.devices)
    fine = Mesh(devices.reshape(4, 2, 8, 4, 4), ("x", "core", "block", "near", "y"))
    rep, shard = ("x", "core"), ("block", "near", "y")
    return jax.shard_map(
        local,
        mesh=fine,
        in_specs=(P(rep, None, shard, None), P(rep, shard, None)),
        out_specs=(P(None, shard, None), P(rep, shard, None)),
        check_vma=False,
    )
```

```python
import functools
import math

import jax
import jax.numpy as jnp
import numpy as np
from jax import lax
from jax.experimental import pallas as pl
from jax.experimental.pallas import tpu as pltpu
from jax.sharding import Mesh
from jax.sharding import PartitionSpec as P

linear_coeff = 3.4445
cubic_coeff = -4.775
quintic_coeff = 2.0315
momentum_rate = 0.9
norm_eps = 1e-06

TILE = 128
HALF = 64
TILES = 5
WIDE = TILE * TILES
GROUPS = 4
ACROSS, BELOW, DIAGONAL, CORNER, PACKED = 512, 768, 1024, 1280, 1408


def places(rows):
    return (lax.broadcasted_iota(jnp.int32, (rows, TILE), axis) for axis in range(2))


def gram_kernel(
    received_ref, momentum_ref, wide_ref, packed_ref, new_ref, momentum, new, read_done, write_done
):
    read = pltpu.make_async_copy(momentum_ref, momentum, read_done)
    read.start()
    summed = received_ref[0].astype(jnp.float32)
    for part in range(1, received_ref.shape[0]):
        summed += received_ref[part].astype(jnp.float32)
    read.wait()
    updated = momentum_rate * momentum[...] + summed
    new[...] = updated
    write = pltpu.make_async_copy(new, new_ref, write_done)
    write.start()
    velocity = (summed + momentum_rate * updated).astype(wide_ref.dtype)
    rows, width = velocity.shape
    padding = jnp.zeros((rows, WIDE - width), wide_ref.dtype)
    wide_ref[...] = jnp.concatenate([velocity, padding], axis=1)

    def tile(i, j):
        return lax.dot_general(
            wide_ref[:, i * TILE : (i + 1) * TILE],
            wide_ref[:, j * TILE : (j + 1) * TILE],
            (((0,), (0,)), ((), ())),
            preferred_element_type=jnp.float32,
        )

    def put(start, block):
        packed_ref[start : start + block.shape[0], :] = block.astype(packed_ref.dtype)

    row, col = places(HALF)
    corner = tile(4, 4)[:HALF]
    for y in range(GROUPS):
        put(y * TILE, tile(y, (y + 1) % 4))
        put(BELOW + y * HALF, tile(4, y)[:HALF])
        square = tile(y, y)
        upper, lower = square[:HALF], square[HALF:]
        moved = jnp.concatenate([lower[:, HALF:], lower[:, :HALF]], axis=1)
        put(DIAGONAL + y * HALF, jnp.where(row > col, moved, upper))
        line = jnp.sum(jnp.where(row == col, moved, 0.0), axis=1, keepdims=True)
        corner = jnp.where(col == HALF + y, line, corner)
    for i in range(2):
        put(ACROSS + i * TILE, tile(i, i + 2))
    put(CORNER, corner)
    put(CORNER + HALF, jnp.zeros((HALF, TILE), jnp.float32))
    write.wait()


def sum_kernel(parts_ref, out_ref):
    total = parts_ref[0].astype(jnp.float32)
    for part in range(1, parts_ref.shape[0]):
        total += parts_ref[part].astype(jnp.float32)
    rounded = total.astype(out_ref.dtype)
    for part in range(out_ref.shape[0]):
        out_ref[part] = rounded


def newton_kernel(factor, packed_ref, rows_ref, out_ref, gram, work, poly):
    zeros = jnp.zeros((HALF, TILE), jnp.float32)
    row, col = places(HALF)

    def part(start, rows):
        return packed_ref[start : start + rows, :].astype(jnp.float32)

    def put(i, j, tile):
        gram[i * TILE : (i + 1) * TILE, j * TILE : (j + 1) * TILE] = tile.astype(gram.dtype)

    def put_both(i, j, tile):
        put(i, j, tile)
        put(j, i, tile.astype(gram.dtype).T)

    corner = part(CORNER, HALF)
    block = jnp.where(col < HALF, corner, 0.0)
    put(4, 4, jnp.concatenate([block, zeros], axis=0))
    trace = jnp.where(row == col, block, 0.0)
    for y in range(GROUPS):
        put_both(y, (y + 1) % 4, part(y * TILE, TILE))
        put_both(4, y, jnp.concatenate([part(BELOW + y * HALF, HALF), zeros], axis=0))
        square = part(DIAGONAL + y * HALF, HALF)
        turned = jnp.concatenate([square, zeros], axis=0).T
        line = jnp.where(col == HALF + y, corner, 0.0)
        trace += jnp.where(row == col, square, 0.0) + line
        line = jnp.sum(line, axis=1, keepdims=True)
        upper = jnp.where(row > col, turned[:HALF], square)
        lower = jnp.where(row > col, square, jnp.where(row < col, turned[:HALF], line))
        lower = jnp.concatenate([turned[HALF:, :HALF], lower[:, :HALF]], axis=1)
        put(y, y, jnp.concatenate([upper, lower], axis=0))
    for i in range(2):
        put_both(i, i + 2, part(ACROSS + i * TILE, TILE))

    total = jnp.sum(trace, axis=(0, 1), keepdims=True)
    inv_norm = 1.0 / (jnp.sqrt(total) + norm_eps)
    inv_square = inv_norm * inv_norm

    def dot(a, b):
        return jnp.dot(a, b, preferred_element_type=jnp.float32)

    edges = [(0, 2 * TILE), (2 * TILE, 4 * TILE), (4 * TILE, WIDE)]

    def symmetric(store, product):
        for start, stop in edges:
            to = min(stop, WIDE - HALF)
            block = product(slice(0, to), slice(start, stop))
            store[0:to, start:stop] = block.astype(store.dtype)
            if start:
                store[start:stop, 0:start] = block[:start].astype(store.dtype).T

    rows = rows_ref[...]
    for store in (poly, work):
        store[WIDE - HALF :, WIDE - TILE :] = jnp.zeros((HALF, TILE), store.dtype)
    symmetric(
        poly,
        lambda to, at: (cubic_coeff * inv_square) * gram[to, at].astype(jnp.float32)
        + (quintic_coeff * inv_square * inv_square) * dot(gram[to, :], gram[:, at]),
    )
    symmetric(
        work,
        lambda to, at: (linear_coeff * inv_square) * gram[to, at].astype(jnp.float32)
        + inv_square * dot(gram[to, :], poly[:, at]),
    )
    first = (linear_coeff * inv_norm) * rows.astype(jnp.float32) + inv_norm * dot(rows, poly[...])
    first = first.astype(jnp.bfloat16)
    symmetric(
        gram,
        lambda to, at: linear_coeff * work[to, at].astype(jnp.float32)
        + dot(poly[to, :], work[:, at]),
    )
    symmetric(
        work,
        lambda to, at: cubic_coeff * gram[to, at].astype(jnp.float32)
        + quintic_coeff * dot(gram[to, :], gram[:, at]),
    )
    result = (linear_coeff * factor) * first.astype(jnp.float32) + factor * dot(first, work[...])
    update = result[:, : out_ref.shape[2]].astype(out_ref.dtype)
    for receiver in range(out_ref.shape[0]):
        out_ref[receiver] = update


VMEM = pl.BlockSpec(memory_space=pltpu.VMEM)
HBM = pl.BlockSpec(memory_space=pl.ANY)
PARAMS = pltpu.CompilerParams(vmem_limit_bytes=32 * 1024 * 1024)


def bf16(*shape):
    return jax.ShapeDtypeStruct(shape, jnp.bfloat16)


def gram(received, momentum):
    rows = momentum.shape[0]
    return pl.pallas_call(
        gram_kernel,
        out_shape=(
            bf16(rows, WIDE),
            bf16(PACKED, TILE),
            jax.ShapeDtypeStruct(momentum.shape, momentum.dtype),
        ),
        in_specs=[VMEM, HBM],
        out_specs=(VMEM, VMEM, HBM),
        scratch_shapes=[pltpu.VMEM(momentum.shape, momentum.dtype)] * 2
        + [pltpu.SemaphoreType.DMA] * 2,
        compiler_params=PARAMS,
    )(received, momentum)


def total_of(parts, receivers):
    return pl.pallas_call(
        sum_kernel,
        out_shape=bf16(receivers, *parts.shape[1:]),
        in_specs=[VMEM],
        out_specs=VMEM,
        compiler_params=PARAMS,
    )(parts)


def newton(factor, packed, wide, width, receivers):
    return pl.pallas_call(
        functools.partial(newton_kernel, factor),
        out_shape=bf16(receivers, wide.shape[0], width),
        in_specs=[VMEM, VMEM],
        out_specs=VMEM,
        scratch_shapes=[pltpu.VMEM((WIDE, WIDE), jnp.bfloat16)] * 3,
        compiler_params=PARAMS,
    )(packed, wide)


def local(partial_grads, momentum):
    rep, cluster = ("x", "core"), ("near", "y")
    blocks = lax.axis_size("block")
    members = lax.axis_size(cluster)
    block_order = sorted(range(blocks), key=lambda block: (block // 2 % 2, block))
    row_count, kv_width = momentum.shape[1:]
    factor = 0.2 * math.sqrt(max(row_count * blocks * members, kv_width))

    received = lax.all_to_all(partial_grads[0], rep, 0, 0, tiled=True)
    wide, packed, new_momentum = gram(received, momentum[0])

    packed = packed.reshape(members, PACKED // members, TILE)
    packed = lax.all_to_all(packed, cluster, 0, 0, tiled=True)
    packed = lax.all_to_all(
        total_of(packed, blocks), "block", 0, 0, axis_index_groups=[block_order], tiled=True
    )
    packed = lax.all_to_all(total_of(packed, members), cluster, 0, 0, tiled=True)
    packed = packed.reshape(PACKED, TILE)

    update = newton(factor, packed, wide, kv_width, lax.axis_size("x"))
    update = lax.all_to_all(update, "x", 0, 0, tiled=True)
    update = lax.all_gather(update, "core", axis=1)
    return (update.reshape(-1, row_count, kv_width), new_momentum[None])


def solution(mesh):
    devices = np.asarray(mesh.devices)
    fine = Mesh(devices.reshape(4, 2, 8, 4, 4), ("x", "core", "block", "near", "y"))
    rep, shard = ("x", "core"), ("block", "near", "y")
    return jax.shard_map(
        local,
        mesh=fine,
        in_specs=(P(rep, None, shard, None), P(rep, shard, None)),
        out_specs=(P(None, shard, None), P(rep, shard, None)),
        check_vma=False,
    )
```
